128 devices in a mesh: group: 8 (over y, core), lend: 16 (over x, z).
Axes of the slice: x: 4, y: 4, z: 4, core: 2. Of those that a mesh axis runs over, the one named last changes fastest.
Arguments:
- tokens: bfloat16 [2, 64, 8192], replicated, may hold values from -6 to 6
- query_weight: bfloat16 [8192, 8192], P('group', 'lend'), may hold values from -0.0625 to 0.0625
- kv_weight: bfloat16 [8192, 2048], P(('group', 'lend')), may hold values from -0.0625 to 0.0625
- pages: bfloat16 [4096, 2, 128, 1024], P(('group', 'lend')), may hold values from -300 to 300
- slot_request: int32 [4096], P(('group', 'lend')), may hold values from 0 to 63
- slot_len: int32 [4096], P(('group', 'lend')), may hold values from 0 to 128, as said below
Outputs:
- attended: bfloat16 [2, 64, 8192], P(None, 'group', 'lend')
The draws below stay inside these ranges and needn't reach their ends.
Inputs may be any that keep to these rules, and one draw needn't show every extreme that they name: `slot_len`: slot lengths are positive exactly in the first slots of each device, at least 16 of them; some device has all 32 slots in use.
All inputs are finite; a program needn't handle non-finite values.
Results may differ from the reference program's by a relative error of at most 0.012.
The reference program's roundings to bfloat16 on the way (of `queries` and `fresh`) count: a program that leaves them out, or rounds other values in their place, can miss the bound.
Values may be sent and summed in bfloat16 or wider, within the bound.
A program may use at most 128 MiB of HBM per device.

```python
import jax
import jax.numpy as jnp
from jax import lax

D = 8192
HQ = 64
KVH = 8
HD = 128
PAGE = 128
STEPS = 2
REQ = 64
PAGES_DEV = 32
N_GROUP = 8
N_LEND = 16


def live_counts(key):
    devices = N_GROUP * N_LEND
    counts = jax.random.randint(jax.random.fold_in(key, 11), (devices,), PAGES_DEV // 2, PAGES_DEV + 1)
    fullest = jax.random.randint(jax.random.fold_in(key, 12), (), 0, devices)
    return jnp.where(jnp.arange(devices) == fullest, PAGES_DEV, counts)


def draw_slot_len(key, part):
    counts = live_counts(key)
    key = jax.random.fold_in(key, 1)
    devices = N_GROUP * N_LEND
    slots = jnp.arange(PAGES_DEV)[None, :]
    partial_len = jax.random.randint(jax.random.fold_in(key, 2), (devices, PAGES_DEV), 1, PAGE + 1)
    chooser = jax.random.randint(jax.random.fold_in(key, 3), (devices, PAGES_DEV), 0, 10)
    lengths = jnp.where(chooser < 3, partial_len, PAGE)
    lengths = jnp.where(slots < counts[:, None], lengths, 0)
    return lengths.reshape(-1).astype(jnp.int32)


def draw_slot_request(key, part):
    key = jax.random.fold_in(key, 2)
    devices = N_GROUP * N_LEND
    drawn = jax.random.randint(key, (devices, PAGES_DEV), 0, REQ)
    slots = jnp.arange(PAGES_DEV)[None, :]
    rows = jnp.arange(devices)[:, None]
    spread = (rows * (PAGES_DEV // 8) + slots) % REQ
    owners = jnp.where(slots < PAGES_DEV // 8, spread, drawn)
    return owners.reshape(-1).astype(jnp.int32)


def draw_pages(key, part):
    key = jax.random.fold_in(key, 3)
    shape = (N_GROUP * N_LEND * PAGES_DEV, 2, PAGE, KVH * HD)
    base = jax.random.normal(key, shape, jnp.float32)
    result = jnp.clip(base, -6.0, 6.0)
    return result.astype(jnp.bfloat16)


def levels(rng, shape, pieces, smallest, top_value):
    factor_of = 1.0
    for axis_at, shards_of in pieces:
        draws = jax.random.uniform(jax.random.fold_in(jax.random.fold_in(rng, 6), axis_at), (shards_of,), jnp.float32, smallest / len(pieces), top_value / len(pieces))
        factor_of = factor_of * jnp.repeat(jnp.exp(draws), shape[axis_at] // shards_of).reshape((-1,) + (1,) * (len(shape) - 1 - axis_at))
    return factor_of


def normal_values(stream_key, shape, scale, bound, pieces=(), kind=jnp.bfloat16):
    values = jax.random.normal(stream_key, shape, jnp.float32) * scale
    if len(pieces) > 0:
        values = levels(stream_key, shape, pieces, -0.22, 0.18) * values
    return jnp.clip(values, min=-bound, max=bound).astype(kind)


def setup_inputs(seed: int = 0) -> dict:
    keys = jax.random.split(jax.random.key(seed), 7)
    return {
        "tokens": normal_values(keys[0], (STEPS, REQ, D), 1.0, 6.0),
        "query_weight": normal_values(keys[1], (D, HQ * HD), D ** -0.5, 0.0625, ((0, 8), (1, 16))),
        "kv_weight": normal_values(keys[2], (D, 2 * KVH * HD), D ** -0.5, 0.0625, ((0, 128),)),
        "pages": draw_pages(jax.random.fold_in(keys[6], 71), 0),
        "slot_request": draw_slot_request(jax.random.fold_in(keys[6], 71), 0),
        "slot_len": draw_slot_len(jax.random.fold_in(keys[6], 71), 0),
    }


def combine_parts(first, second):
    maxima = jnp.maximum(first[0], second[0])
    left = jnp.exp(first[0] - maxima)
    right = jnp.exp(second[0] - maxima)
    totals = first[1] * left + second[1] * right
    weighted = first[2] * left[..., None] + second[2] * right[..., None]
    return (maxima, totals, weighted)

def page_partial(queries, page_rows, owners, lengths, page_ok, requests):
    count = page_rows.shape[0]
    key_rows = page_rows[:, 0].reshape(count, PAGE, KVH, HD).astype(jnp.float32)
    value_rows = page_rows[:, 1].reshape(count, PAGE, KVH, HD).astype(jnp.float32)
    chosen = jnp.take(queries, owners, axis=0).astype(jnp.float32)
    scores = jnp.einsum('pkgd,ptkd->pkgt', chosen, key_rows, precision=lax.Precision.HIGHEST) / jnp.sqrt(jnp.float32(HD))
    positions = jnp.arange(PAGE, dtype=jnp.int32)
    valid = page_ok[:, None, None, None] & (positions[None, None, None, :] < lengths[:, None, None, None])
    owned = (owners[:, None] == jnp.arange(requests, dtype=jnp.int32)[None, :]) & page_ok[:, None]
    page_max = lax.optimization_barrier(jnp.max(jnp.where(valid, scores, -1e+30), axis=3))
    maxima = lax.optimization_barrier(jnp.max(jnp.where(owned[:, :, None, None], page_max[:, None], -1e+30), axis=0))
    anchor = jnp.take(maxima, owners, axis=0)
    weights = jnp.where(valid, jnp.exp(scores - anchor[..., None]), 0.0)
    owned_float = owned.astype(jnp.float32)
    totals = jnp.einsum('pr,pkg->rkg', owned_float, lax.optimization_barrier(jnp.sum(weights, axis=3)), precision=lax.Precision.HIGHEST)
    per_page = jnp.einsum('pkgt,ptkd->pkgd', weights, value_rows, precision=lax.Precision.HIGHEST)
    weighted = jnp.einsum('pr,pkgd->rkgd', owned_float, per_page, precision=lax.Precision.HIGHEST)
    return (maxima, totals, weighted)

def fresh_partial(queries, fresh, owned):
    count = fresh.shape[0]
    requests = fresh.shape[1]
    key_rows = fresh[:, :, :KVH * HD].reshape(count, requests, KVH, HD).astype(jnp.float32)
    value_rows = fresh[:, :, KVH * HD:].reshape(count, requests, KVH, HD).astype(jnp.float32)
    scores = jnp.einsum('rkgd,trkd->rkgt', queries.astype(jnp.float32), key_rows, precision=lax.Precision.HIGHEST) / jnp.sqrt(jnp.float32(HD))
    maxima = jnp.where(owned[:, None, None], lax.optimization_barrier(jnp.max(scores, axis=3)), -1e+30)
    weights = jnp.where(owned[:, None, None, None], jnp.exp(scores - maxima[..., None]), 0.0)
    weighted = jnp.einsum('rkgt,trkd->rkgd', weights, value_rows, precision=lax.Precision.HIGHEST)
    return (maxima, lax.optimization_barrier(jnp.sum(weights, axis=3)), weighted)

def reference(tokens, query_weight, kv_weight, pages, slot_request, slot_len):
    devices = N_GROUP * N_LEND
    grouped = HQ // KVH
    fresh = jnp.dot(tokens.reshape(STEPS * REQ, D), kv_weight, preferred_element_type=jnp.float32)
    fresh = fresh.astype(jnp.bfloat16).reshape(STEPS, REQ, 2 * KVH * HD)
    device_pages = pages.reshape(devices, PAGES_DEV, 2, PAGE, KVH * HD)
    device_owner = slot_request.reshape(devices, PAGES_DEV)
    device_len = slot_len.reshape(devices, PAGES_DEV)
    results = []
    for step_index in range(STEPS):
        queries = jnp.dot(tokens[step_index], query_weight, preferred_element_type=jnp.float32)
        queries = queries.astype(jnp.bfloat16).reshape(REQ, KVH, grouped, HD)
        start = (jnp.full((REQ, KVH, grouped), -1e+30, jnp.float32), jnp.zeros((REQ, KVH, grouped), jnp.float32), jnp.zeros((REQ, KVH, grouped, HD), jnp.float32))

        def visit(carried, visited):
            page_rows, owners, lengths = visited
            part = page_partial(queries, page_rows, owners, lengths, lengths > 0, REQ)
            return (combine_parts(carried, part), None)
        carried, unused = lax.scan(visit, start, (device_pages, device_owner, device_len))
        everyone = jnp.ones((REQ,), dtype=bool)
        carried = combine_parts(carried, fresh_partial(queries, fresh[:step_index + 1], everyone))
        output = carried[2] / carried[1][..., None]
        results.append(output.astype(jnp.bfloat16).reshape(REQ, HQ * HD))
    return jnp.stack(results)
```

```python
import functools

import jax
import jax.numpy as jnp
from jax import lax
from jax.experimental import pallas as pl
from jax.experimental.pallas import tpu as pltpu
from jax.sharding import PartitionSpec as P

HD = 128
CORES = 2
NEG = -1e30
LOG2E = 1.4426950408889634
MESH = pl.DeviceIdType.MESH
F32 = jnp.float32
BF16 = jnp.bfloat16
UNROLL = 8

(S_KVW, S_OWN, S_RS, S_FRS, S_KEY, S_VAL, S_G1, S_G2, S_H1, S_H2, S_SIB,
 S_E, S_EL, S_F, S_FL) = range(15)
L_TOK, L_WQ, L_KV, L_PAGES = range(4)


def kernel(ng, nl, tok, wq, kvw, pages, own_s, len_s, out,
           tok_v, wq_v, wkv_v, pages_v, qpart, rs, fpart, frs, kvown, kv_r, q_all,
           own_b, eo, slot_o, res, res_l, er, el, ff, fb, fl, fr, frl, qf,
           send, recv, local):
    g = lax.axis_index("group")
    l = lax.axis_index("lend")
    y, c = g // CORES, g % CORES
    ny = ng // CORES
    h_own, par = l // 2, l % 2
    kvh = nl // 2
    nch = 2 * ng
    slots = pages.shape[0]
    page = pages.shape[2]
    steps, req, rows = tok_v.shape
    kvrows = kvw.shape[0]

    def copy(src, dst, which, gg, ll):
        return pltpu.make_async_remote_copy(
            src_ref=src, dst_ref=dst, send_sem=send.at[which], recv_sem=recv.at[which],
            device_id=(gg, ll), device_id_type=MESH)

    def wait_all(ref, sem):
        pltpu.make_async_copy(ref, ref, sem).wait()

    def each(n, body):
        def step(k, carry):
            body(k)
            return carry
        lax.fori_loop(1, n, step, 0)

    c_tok = pltpu.make_async_copy(tok.at[:, :, pl.ds(pl.multiple_of(g * rows, 128), rows)], tok_v, local.at[L_TOK])
    c_tok.start()
    c_wq = pltpu.make_async_copy(wq, wq_v, local.at[L_WQ])
    c_wq.start()
    c_kv = pltpu.make_async_copy(
        kvw.at[:, pl.ds(pl.multiple_of(l * HD, HD), HD)],
        wkv_v.at[pl.ds(pl.multiple_of(l * kvrows, kvrows), kvrows)], local.at[L_KV])
    c_kv.start()

    barrier = pltpu.get_barrier_semaphore()

    def greet(gg, ll):
        pl.semaphore_signal(barrier, inc=1, device_id=(gg, ll), device_id_type=MESH)

    each(nl, lambda k: greet(g, lax.rem(l + k, nl)))

    def greet_group(k):
        gg = lax.rem(g + k, ng)
        greet(gg, l)
        greet(gg, h_own * 2 + (1 - par))
    each(ng, greet_group)

    def start_pages(k, carry):
        pltpu.make_async_copy(pages.at[pl.ds(k * 2, 2)], pages_v.at[pl.ds(k * 2, 2)], local.at[L_PAGES]).start()
        return carry
    lax.fori_loop(0, slots // 2, start_pages, 0)

    lane = lax.broadcasted_iota(jnp.int32, (8, 128), 1)
    quarter = (l % 4) * slots
    owners = jnp.full((8, 128), -1, jnp.int32)
    for p in range(slots):
        owners = jnp.where(lane == quarter + p, own_s[p], owners)
    own_b[...] = owners
    eo[l] = owners

    pl.semaphore_wait(barrier, (nl - 1) + 2 * (ng - 1))

    def send_kv(k):
        ll = lax.rem(l + k, nl)
        copy(kvw.at[:, pl.ds(pl.multiple_of(ll * HD, HD), HD)],
             wkv_v.at[pl.ds(pl.multiple_of(l * kvrows, kvrows), kvrows)], S_KVW, g, ll).start()
        copy(own_b, eo.at[l], S_OWN, g, ll).start()
    each(nl, send_kv)

    c_tok.wait()
    tokens = tok_v[...].reshape(steps * req, rows)
    to = lax.broadcasted_iota(jnp.int32, (steps * req, steps * req), 0)
    fro = lax.broadcasted_iota(jnp.int32, (steps * req, steps * req), 1)
    source = ((to // 4) % 2) * req + (to // 8) * 4 + to % 4
    order = jnp.where(fro == source, 1.0, 0.0).astype(BF16)
    ordered = jnp.dot(order, tokens, preferred_element_type=F32).astype(BF16)
    c_wq.wait()
    part = jnp.dot(ordered, wq_v[...], preferred_element_type=F32)
    qpart[...] = part.reshape(nch, 8, 4 * HD)
    mine = g * 2 + par
    rs[mine] = qpart[mine]

    def send_rs(k):
        idx = lax.rem(mine + k, nch)
        copy(qpart.at[idx], rs.at[mine], S_RS, idx // 2, h_own * 2 + idx % 2).start()
    each(nch, send_rs)

    c_kv.wait()
    wait_all(wkv_v.at[pl.ds(0, (nl - 1) * kvrows)], recv.at[S_KVW])
    fpart[...] = jnp.dot(tokens, wkv_v[...], preferred_element_type=F32).reshape(steps, req, HD)
    frs[g] = fpart[:, pl.ds(pl.multiple_of(g * 8, 8), 8), :]

    def send_frs(k):
        gg = lax.rem(g + k, ng)
        copy(fpart.at[:, pl.ds(pl.multiple_of(gg * 8, 8), 8), :], frs.at[g], S_FRS, gg, l).start()
    each(ng, send_frs)

    wait_all(rs.at[pl.ds(0, nch - 1)], recv.at[S_RS])
    blocks = []
    for half in range(2):
        total = rs[half]
        for gg in range(1, ng):
            total = total + rs[2 * gg + half]
        for j in range(4):
            blocks.append(total[:, j * HD:(j + 1) * HD])
    stacked = jnp.concatenate(blocks, axis=0).astype(BF16)
    to = lax.broadcasted_iota(jnp.int32, (64, 64), 0)
    fro = lax.broadcasted_iota(jnp.int32, (64, 64), 1)
    source = ((to // 8) % 2) * 32 + (to % 4) * 8 + ((to // 4) % 2) * 4 + to // 16
    order = jnp.where(fro == source, 1.0, 0.0).astype(BF16)
    chunk = jnp.dot(order, stacked, preferred_element_type=F32).astype(BF16)
    first = 8 * c + 4 * par
    q_all[h_own, y, pl.ds(first, 4)] = chunk.reshape(4, 16, HD)

    piece1 = q_all.at[h_own, y, pl.ds(first, 2)]
    piece2 = q_all.at[h_own, y, pl.ds(first + 2, 2)]

    def send_g2(k):
        copy(piece2, piece2, S_G2, lax.rem(y + k, ny) * CORES + c, l).start()
    each(ny, send_g2)

    def send_g1(k):
        copy(piece1, piece1, S_G1, g, lax.rem(l + k, nl)).start()
    each(nl, send_g1)

    wait_all(q_all.at[pl.ds(0, 2), 0, pl.ds(0, ny - 1)], recv.at[S_G2])

    def send_h2(k):
        block = q_all.at[h_own, :, pl.ds(first + 2, 2)]
        copy(block, block, S_H2, g, lax.rem(l + k, nl)).start()
    each(nl, send_h2)

    wait_all(q_all.at[pl.ds(0, 2), 0, pl.ds(0, nl - 1)], recv.at[S_G1])

    def send_h1(k):
        gg = lax.rem(y + k, ny) * CORES + c
        for pp in range(2):
            block = q_all.at[:, y, pl.ds(8 * c + 4 * pp, 2)]
            copy(block, block, S_H1, gg, l).start()
    each(ny, send_h1)

    wait_all(frs.at[pl.ds(0, ng - 1)], recv.at[S_FRS])
    total = frs[0]
    for gg in range(1, ng):
        total = total + frs[gg]
    kvown[...] = total.reshape(steps * 8, HD).astype(BF16)
    which = l // kvh
    for pp in range(2):
        ll = (l % kvh) * 2 + pp

        @pl.when(ll == l)
        def _():
            kv_r[which] = kvown[...]

        for kind in range(2):
            @pl.when((ll != l) & (which == kind))
            def _():
                copy(kvown, kv_r.at[kind], S_KEY + kind, g, ll).start()

    wait_all(q_all.at[:, pl.ds(0, ny - 1), pl.ds(0, 4)], recv.at[S_H1])
    for pp in range(2):
        block = q_all.at[:, :, pl.ds(8 * c + 4 * pp, 2)]
        copy(block, block, S_SIB, y * CORES + (1 - c), l).start()
    wait_all(q_all.at[:, 0, pl.ds(0, (nl - 1) * ny * 2 // kvh)], recv.at[S_H2])
    for pp in range(2):
        block = q_all.at[:, :, pl.ds(8 * c + 4 * pp + 2, 2)]
        copy(block, block, S_SIB, y * CORES + (1 - c), l).start()
    wait_all(q_all.at[:, :, pl.ds(0, 8)], recv.at[S_SIB])
    wait_all(pages_v, local.at[L_PAGES])

    scale = LOG2E / (HD ** 0.5)
    lane16 = lax.broadcasted_iota(jnp.int32, (16, 128), 1)

    def head(i, carry):
        h = lax.rem(h_own + 1 + i, kvh)
        columns = pl.ds(pl.multiple_of(h * HD, HD), HD)

        def visit(b, state):
            maxima, sums = state
            for u in range(UNROLL):
                p = b * UNROLL + u
                r = own_s[p]
                query = q_all[h, r // 16, r % 16]
                keys = pages_v[p, 0, :, columns]
                values = pages_v[p, 1, :, columns]
                s = lax.dot_general(query, keys, (((1,), (1,)), ((), ())), preferred_element_type=F32) * scale
                ok = lane16 < len_s[p]
                s = jnp.where(ok, s, NEG)
                m = jnp.max(s, axis=1, keepdims=True)
                w = jnp.where(ok, jnp.exp2(s - m), 0.0)
                t = jnp.sum(w, axis=1, keepdims=True)
                o = jnp.dot(w.astype(BF16), values, preferred_element_type=F32)
                o = o / jnp.maximum(t, 1e-30)
                slot_o[pl.ds(p, 16, stride=slots), :] = o
                here = lane16 == quarter + p
                maxima = jnp.where(here, m, maxima)
                sums = jnp.where(here, t, sums)
            return maxima, sums

        maxima, sums = lax.fori_loop(
            0, slots // UNROLL, visit,
            (jnp.full((16, 128), NEG, F32), jnp.zeros((16, 128), F32)))
        lse = jnp.where(sums > 0.0, maxima + jnp.log(jnp.maximum(sums, 1e-30)) * LOG2E, NEG)
        for half in range(2):
            ll = 2 * h + half
            res[ll] = slot_o[pl.ds(half * 8 * slots, 8 * slots), :].astype(BF16)
            res_l[ll] = lse[half * 8:(half + 1) * 8]

            @pl.when(ll != l)
            def _():
                copy(res.at[ll], er.at[l], S_E, g, ll).start()
                copy(res_l.at[ll], el.at[l], S_EL, g, ll).start()

            @pl.when(ll == l)
            def _():
                er[l] = res[ll]
                el[l] = res_l[ll]
        return carry

    lax.fori_loop(0, kvh, head, 0)

    qf[...] = q_all[h_own, y, pl.ds(8 * c, 8)].reshape(128, HD).astype(F32)

    @pl.when(l != h_own)
    def _():
        wait_all(kv_r.at[0], recv.at[S_KEY])

    @pl.when(l != kvh + h_own)
    def _():
        wait_all(kv_r.at[1], recv.at[S_VAL])

    fresh_k = kv_r[0].astype(F32)
    fresh_v = kv_r[1].astype(F32)
    fresh_scores = []
    for i in range(8):
        q_i = qf[pl.ds(par * 8 + i, 8, stride=16), :]
        fresh_scores.append([
            jnp.sum(q_i * fresh_k[t * 8:(t + 1) * 8], axis=1, keepdims=True) * scale
            for t in range(i // 4 + 1)])

    wait_all(eo.at[pl.ds(0, nl - 1)], recv.at[S_OWN])
    wait_all(el.at[pl.ds(0, nl - 1)], recv.at[S_EL])
    wait_all(er.at[pl.ds(0, nl - 1)], recv.at[S_E])
    request = lax.broadcasted_iota(jnp.int32, (req, 128), 0)
    owned, logs = [], []
    for k in range(nl // 4):
        o, s = eo[4 * k], el[4 * k]
        for x in range(1, 4):
            o = jnp.maximum(o, eo[4 * k + x])
            s = jnp.maximum(s, el[4 * k + x])
        owned.append(o[0:1] == request)
        logs.append(s)
    laneq = lax.broadcasted_iota(jnp.int32, (req, 128), 1)
    lse_out = jnp.full((req, 128), NEG, F32)
    for i in range(8):
        masked = [jnp.where(owned[k], logs[k][i:i + 1], NEG) for k in range(nl // 4)]
        m = masked[0]
        for k in range(1, nl // 4):
            m = jnp.maximum(m, masked[k])
        m = jnp.max(m, axis=1, keepdims=True)
        weights = [jnp.where(x > 0.5 * NEG, jnp.exp2(x - m), 0.0) for x in masked]
        t = weights[0]
        for k in range(1, nl // 4):
            t = t + weights[k]
        t = jnp.sum(t, axis=1, keepdims=True)
        weights = jnp.concatenate(weights, axis=1).astype(BF16)
        data = er[:, i * slots:(i + 1) * slots, :].reshape(nl * slots, HD)
        o = jnp.dot(weights, data, preferred_element_type=F32) / jnp.maximum(t, 1e-30)
        ff[:, i * 8:(i + 1) * 8, :] = o.reshape(ng, 8, HD)
        lse = jnp.where(t > 0.0, m + jnp.log(jnp.maximum(t, 1e-30)) * LOG2E, NEG)
        lse_out = jnp.where(laneq == i, lse, lse_out)
    fb[...] = ff[...].astype(BF16)
    fl[...] = lse_out.reshape(ng, 8, 128)
    fr[g] = fb[g]
    frl[g] = fl[g]

    def send_f(k):
        gg = lax.rem(g + k, ng)
        copy(fb.at[gg], fr.at[g], S_F, gg, l).start()
        copy(fl.at[gg], frl.at[g], S_FL, gg, l).start()
    each(ng, send_f)

    wait_all(frl.at[pl.ds(0, ng - 1)], recv.at[S_FL])
    wait_all(fr.at[pl.ds(0, ng - 1)], recv.at[S_F])
    data = [fr[gg].astype(F32) for gg in range(ng)]
    logs = [frl[gg] for gg in range(ng)]
    for s in range(steps):
        pieces = []
        for j in range(4):
            i = s * 4 + j
            parts = [(logs[gg][:, i:i + 1], data[gg][i * 8:(i + 1) * 8]) for gg in range(ng)]
            parts += [(fresh_scores[i][t], fresh_v[t * 8:(t + 1) * 8]) for t in range(s + 1)]
            m = parts[0][0]
            for score, unused in parts[1:]:
                m = jnp.maximum(m, score)
            total = jnp.zeros((8, 1), F32)
            o = jnp.zeros((8, HD), F32)
            for score, value in parts:
                w = jnp.exp2(score - m)
                total = total + w
                o = o + w * value
            pieces.append(o / total)
        out[s] = jnp.concatenate(pieces, axis=1).astype(BF16)

    wait_all(wkv_v.at[pl.ds(0, (nl - 1) * kvrows)], send.at[S_KVW])
    wait_all(eo.at[pl.ds(0, nl - 1)], send.at[S_OWN])
    wait_all(rs.at[pl.ds(0, nch - 1)], send.at[S_RS])
    wait_all(frs.at[pl.ds(0, ng - 1)], send.at[S_FRS])
    wait_all(q_all.at[pl.ds(0, 2), 0, pl.ds(0, nl - 1)], send.at[S_G1])
    wait_all(q_all.at[pl.ds(0, 2), 0, pl.ds(0, ny - 1)], send.at[S_G2])
    wait_all(q_all.at[:, pl.ds(0, ny - 1), pl.ds(0, 4)], send.at[S_H1])
    wait_all(q_all.at[:, 0, pl.ds(0, (nl - 1) * ny * 2 // kvh)], send.at[S_H2])
    wait_all(q_all.at[:, :, pl.ds(0, 8)], send.at[S_SIB])
    for kind in range(2):
        for pp in range(2):
            @pl.when((which == kind) & ((l % kvh) * 2 + pp != l))
            def _():
                wait_all(kvown, send.at[S_KEY + kind])
    wait_all(er.at[pl.ds(0, nl - 1)], send.at[S_E])
    wait_all(el.at[pl.ds(0, nl - 1)], send.at[S_EL])
    wait_all(fr.at[pl.ds(0, ng - 1)], send.at[S_F])
    wait_all(frl.at[pl.ds(0, ng - 1)], send.at[S_FL])


def per_device(ng, nl, tokens, query_weight, kv_weight, pages, slot_request, slot_len):
    steps, req, width = tokens.shape
    rows = query_weight.shape[0]
    slots, unused, page, kvwidth = pages.shape
    kvh = kvwidth // HD
    ny = ng // CORES
    hbm = pl.BlockSpec(memory_space=pl.ANY)
    smem = pl.BlockSpec(memory_space=pltpu.SMEM)
    scratch = [
        pltpu.VMEM((steps, req, rows), BF16),
        pltpu.VMEM((rows, 4 * HD), BF16),
        pltpu.VMEM((rows, HD), BF16),
        pltpu.VMEM(pages.shape, BF16),
        pltpu.VMEM((2 * ng, 8, 4 * HD), F32),
        pltpu.VMEM((2 * ng, 8, 4 * HD), F32),
        pltpu.VMEM((steps, req, HD), F32),
        pltpu.VMEM((ng, steps, 8, HD), F32),
        pltpu.VMEM((steps * 8, HD), BF16),
        pltpu.VMEM((2, steps * 8, HD), BF16),
        pltpu.VMEM((kvh, ny, 16, 16, HD), BF16),
        pltpu.VMEM((8, 128), jnp.int32),
        pltpu.VMEM((nl, 8, 128), jnp.int32),
        pltpu.VMEM((16 * slots, HD), F32),
        pltpu.VMEM((nl, 8 * slots, HD), BF16),
        pltpu.VMEM((nl, 8, 128), F32),
        pltpu.VMEM((nl, 8 * slots, HD), BF16),
        pltpu.VMEM((nl, 8, 128), F32),
        pltpu.VMEM((ng, 64, HD), F32),
        pltpu.VMEM((ng, 64, HD), BF16),
        pltpu.VMEM((ng, 8, 128), F32),
        pltpu.VMEM((ng, 64, HD), BF16),
        pltpu.VMEM((ng, 8, 128), F32),
        pltpu.VMEM((128, HD), F32),
        pltpu.SemaphoreType.DMA((15,)),
        pltpu.SemaphoreType.DMA((15,)),
        pltpu.SemaphoreType.DMA((4,)),
    ]
    return pl.pallas_call(
        functools.partial(kernel, ng, nl),
        out_shape=jax.ShapeDtypeStruct((steps, req // ng, 4 * HD), BF16),
        in_specs=[hbm, hbm, hbm, hbm, smem, smem],
        out_specs=pl.BlockSpec(memory_space=pltpu.VMEM),
        scratch_shapes=scratch,
        compiler_params=pltpu.CompilerParams(
            collective_id=0, has_side_effects=True, vmem_limit_bytes=48 * 1024 * 1024),
    )(tokens, query_weight, kv_weight, pages, slot_request, slot_len)


def solution(mesh):
    ng, nl = mesh.shape["group"], mesh.shape["lend"]
    return jax.shard_map(
        functools.partial(per_device, ng, nl),
        mesh=mesh,
        in_specs=(
            P(),
            P("group", "lend"),
            P(("group", "lend"), None),
            P(("group", "lend"), None, None, None),
            P(("group", "lend")),
            P(("group", "lend")),
        ),
        out_specs=P(None, "group", "lend"),
        check_vma=False,
    )
```

```python
import functools

import jax
import jax.numpy as jnp
from jax import lax
from jax.experimental import pallas as pl
from jax.experimental.pallas import tpu as pltpu
from jax.sharding import PartitionSpec as P

HD = 128
CORES = 2
NEG = -1e30
LOG2E = 1.4426950408889634
MESH = pl.DeviceIdType.MESH
F32 = jnp.float32
BF16 = jnp.bfloat16
UNROLL = 16

(S_KVW, S_OWN, S_RS, S_FRS, S_KEY, S_VAL, S_G1, S_G2, S_H1, S_H2, S_SIB,
 S_E, S_EL, S_F, S_FL) = range(15)
L_TOK, L_WQ, L_KV, L_PAGES = range(4)


def kernel(ng, nl, tok, wq, kvw, pages, own_s, len_s, out,
           tok_v, wq_v, wkv_v, pages_v, qpart, rs, fpart, frs, kvown, kv_r, q_all,
           own_b, eo, slot_o, res, res_l, er, el, ff, fb, fl, fr, frl, qf,
           send, recv, local):
    g = lax.axis_index("group")
    l = lax.axis_index("lend")
    y, c = g // CORES, g % CORES
    ny = ng // CORES
    h_own, par = l // 2, l % 2
    kvh = nl // 2
    nch = 2 * ng
    slots = pages.shape[0]
    page = pages.shape[2]
    steps, req, rows = tok_v.shape
    kvrows = kvw.shape[0]

    def copy(src, dst, which, gg, ll):
        return pltpu.make_async_remote_copy(
            src_ref=src, dst_ref=dst, send_sem=send.at[which], recv_sem=recv.at[which],
            device_id=(gg, ll), device_id_type=MESH)

    def wait_all(ref, sem):
        pltpu.make_async_copy(ref, ref, sem).wait()

    def each(n, body):
        def step(k, carry):
            body(k)
            return carry
        lax.fori_loop(1, n, step, 0)

    c_tok = pltpu.make_async_copy(tok.at[:, :, pl.ds(pl.multiple_of(g * rows, 128), rows)], tok_v, local.at[L_TOK])
    c_tok.start()
    c_wq = pltpu.make_async_copy(wq, wq_v, local.at[L_WQ])
    c_wq.start()
    c_kv = pltpu.make_async_copy(
        kvw.at[:, pl.ds(pl.multiple_of(l * HD, HD), HD)],
        wkv_v.at[pl.ds(pl.multiple_of(l * kvrows, kvrows), kvrows)], local.at[L_KV])
    c_kv.start()

    barrier = pltpu.get_barrier_semaphore()

    def greet(gg, ll):
        pl.semaphore_signal(barrier, inc=1, device_id=(gg, ll), device_id_type=MESH)

    each(nl, lambda k: greet(g, lax.rem(l + k, nl)))

    def greet_group(k):
        gg = lax.rem(g + k, ng)
        greet(gg, l)
        greet(gg, h_own * 2 + (1 - par))
    each(ng, greet_group)

    def start_pages(k, carry):
        pltpu.make_async_copy(pages.at[pl.ds(k * 2, 2)], pages_v.at[pl.ds(k * 2, 2)], local.at[L_PAGES]).start()
        return carry
    lax.fori_loop(0, slots // 2, start_pages, 0)

    c_tok.wait()
    tokens = tok_v[...].reshape(steps * req, rows)
    to = lax.broadcasted_iota(jnp.int32, (steps * req, steps * req), 0)
    fro = lax.broadcasted_iota(jnp.int32, (steps * req, steps * req), 1)
    source = ((to // 4) % 2) * req + (to // 8) * 4 + to % 4
    order = jnp.where(fro == source, 1.0, 0.0).astype(BF16)
    ordered = jnp.dot(order, tokens, preferred_element_type=F32).astype(BF16)
    c_wq.wait()
    part = jnp.dot(ordered, wq_v[...], preferred_element_type=F32)
    qpart[...] = part.reshape(nch, 8, 4 * HD)
    mine = g * 2 + par
    rs[mine] = qpart[mine]

    pl.semaphore_wait(barrier, (nl - 1) + 2 * (ng - 1))

    def send_rs(k):
        idx = lax.rem(mine + k, nch)
        copy(qpart.at[idx], rs.at[mine], S_RS, idx // 2, h_own * 2 + idx % 2).start()
    each(nch, send_rs)

    def send_kv(k):
        ll = lax.rem(l + k, nl)
        copy(kvw.at[:, pl.ds(pl.multiple_of(ll * HD, HD), HD)],
             wkv_v.at[pl.ds(pl.multiple_of(l * kvrows, kvrows), kvrows)], S_KVW, g, ll).start()
    each(nl, send_kv)

    wait_all(rs.at[pl.ds(0, nch - 1)], recv.at[S_RS])
    blocks = []
    for half in range(2):
        total = rs[half]
        for gg in range(1, ng):
            total = total + rs[2 * gg + half]
        for j in range(4):
            blocks.append(total[:, j * HD:(j + 1) * HD])
    stacked = jnp.concatenate(blocks, axis=0).astype(BF16)
    to = lax.broadcasted_iota(jnp.int32, (64, 64), 0)
    fro = lax.broadcasted_iota(jnp.int32, (64, 64), 1)
    source = ((to // 8) % 2) * 32 + (to % 4) * 8 + ((to // 4) % 2) * 4 + to // 16
    order = jnp.where(fro == source, 1.0, 0.0).astype(BF16)
    chunk = jnp.dot(order, stacked, preferred_element_type=F32).astype(BF16)
    first = 8 * c + 4 * par
    q_all[h_own, y, pl.ds(first, 4)] = chunk.reshape(4, 16, HD)

    piece1 = q_all.at[h_own, y, pl.ds(first, 2)]
    piece2 = q_all.at[h_own, y, pl.ds(first + 2, 2)]

    def send_g2(k):
        copy(piece2, piece2, S_G2, lax.rem(y + k, ny) * CORES + c, l).start()
    each(ny, send_g2)

    def send_g1(k):
        copy(piece1, piece1, S_G1, g, lax.rem(l + k, nl)).start()
    each(nl, send_g1)

    c_kv.wait()
    wait_all(wkv_v.at[pl.ds(0, (nl - 1) * kvrows)], recv.at[S_KVW])
    fpart[...] = jnp.dot(tokens, wkv_v[...], preferred_element_type=F32).reshape(steps, req, HD)
    frs[g] = fpart[:, pl.ds(pl.multiple_of(g * 8, 8), 8), :]

    def send_frs(k):
        gg = lax.rem(g + k, ng)
        copy(fpart.at[:, pl.ds(pl.multiple_of(gg * 8, 8), 8), :], frs.at[g], S_FRS, gg, l).start()
    each(ng, send_frs)

    wait_all(q_all.at[pl.ds(0, 2), 0, pl.ds(0, ny - 1)], recv.at[S_G2])

    def send_h2(k):
        block = q_all.at[h_own, :, pl.ds(first + 2, 2)]
        copy(block, block, S_H2, g, lax.rem(l + k, nl)).start()
    each(nl, send_h2)

    wait_all(q_all.at[pl.ds(0, 2), 0, pl.ds(0, nl - 1)], recv.at[S_G1])

    def send_h1(k):
        gg = lax.rem(y + k, ny) * CORES + c
        for pp in range(2):
            block = q_all.at[:, y, pl.ds(8 * c + 4 * pp, 2)]
            copy(block, block, S_H1, gg, l).start()
    each(ny, send_h1)

    lane = lax.broadcasted_iota(jnp.int32, (8, 128), 1)
    quarter = (l % 4) * slots
    owners = jnp.full((8, 128), -1, jnp.int32)
    for p in range(slots):
        owners = jnp.where(lane == quarter + p, own_s[p], owners)
    own_b[...] = owners
    eo[l] = owners

    each(nl, lambda k: copy(own_b, eo.at[l], S_OWN, g, lax.rem(l + k, nl)).start())

    wait_all(q_all.at[:, pl.ds(0, ny - 1), pl.ds(0, 4)], recv.at[S_H1])
    for pp in range(2):
        block = q_all.at[:, :, pl.ds(8 * c + 4 * pp, 2)]
        copy(block, block, S_SIB, y * CORES + (1 - c), l).start()
    wait_all(q_all.at[:, 0, pl.ds(0, (nl - 1) * ny * 2 // kvh)], recv.at[S_H2])
    for pp in range(2):
        block = q_all.at[:, :, pl.ds(8 * c + 4 * pp + 2, 2)]
        copy(block, block, S_SIB, y * CORES + (1 - c), l).start()

    wait_all(frs.at[pl.ds(0, ng - 1)], recv.at[S_FRS])
    total = frs[0]
    for gg in range(1, ng):
        total = total + frs[gg]
    kvown[...] = total.reshape(steps * 8, HD).astype(BF16)
    which = l // kvh
    for pp in range(2):
        ll = (l % kvh) * 2 + pp

        @pl.when(ll == l)
        def _():
            kv_r[which] = kvown[...]

        for kind in range(2):
            @pl.when((ll != l) & (which == kind))
            def _():
                copy(kvown, kv_r.at[kind], S_KEY + kind, g, ll).start()

    wait_all(q_all.at[:, :, pl.ds(0, 8)], recv.at[S_SIB])
    wait_all(pages_v, local.at[L_PAGES])

    scale = LOG2E / (HD ** 0.5)
    lane16 = lax.broadcasted_iota(jnp.int32, (16, 128), 1)

    def head(i, carry):
        h = lax.rem(h_own + 1 + i, kvh)
        columns = pl.ds(pl.multiple_of(h * HD, HD), HD)

        def visit(b, state):
            maxima, sums = state
            block = [b * UNROLL + u for u in range(UNROLL)]
            scores = []
            for p in block:
                r = own_s[p]
                scores.append(lax.dot_general(
                    q_all[h, r // 16, r % 16], pages_v[p, 0, :, columns],
                    (((1,), (1,)), ((), ())), preferred_element_type=F32) * scale)
            valid = [lane16 < len_s[p] for p in block]
            scores = [jnp.where(ok, x, NEG) for ok, x in zip(valid, scores)]
            tops = [jnp.max(x, axis=1, keepdims=True) for x in scores]
            weights = [jnp.where(ok, jnp.exp2(x - m), 0.0) for ok, x, m in zip(valid, scores, tops)]
            totals = [jnp.sum(w, axis=1, keepdims=True) for w in weights]
            outs = [
                jnp.dot(w.astype(BF16), pages_v[p, 1, :, columns], preferred_element_type=F32)
                for w, p in zip(weights, block)]
            for p, o, m, t in zip(block, outs, tops, totals):
                slot_o[pl.ds(p, 16, stride=slots), :] = o / jnp.maximum(t, 1e-30)
                here = lane16 == quarter + p
                maxima = jnp.where(here, m, maxima)
                sums = jnp.where(here, t, sums)
            return maxima, sums

        maxima, sums = lax.fori_loop(
            0, slots // UNROLL, visit,
            (jnp.full((16, 128), NEG, F32), jnp.zeros((16, 128), F32)))
        lse = jnp.where(sums > 0.0, maxima + jnp.log(jnp.maximum(sums, 1e-30)) * LOG2E, NEG)
        for half in range(2):
            ll = 2 * h + half
            res[ll] = slot_o[pl.ds(half * 8 * slots, 8 * slots), :].astype(BF16)
            res_l[ll] = lse[half * 8:(half + 1) * 8]

            @pl.when(ll != l)
            def _():
                copy(res.at[ll], er.at[l], S_E, g, ll).start()
                copy(res_l.at[ll], el.at[l], S_EL, g, ll).start()

            @pl.when(ll == l)
            def _():
                er[l] = res[ll]
                el[l] = res_l[ll]
        return carry

    lax.fori_loop(0, kvh, head, 0)

    qf[...] = q_all[h_own, y, pl.ds(8 * c, 8)].reshape(128, HD).astype(F32)

    @pl.when(l != h_own)
    def _():
        wait_all(kv_r.at[0], recv.at[S_KEY])

    @pl.when(l != kvh + h_own)
    def _():
        wait_all(kv_r.at[1], recv.at[S_VAL])

    fresh_k = kv_r[0].astype(F32)
    fresh_v = kv_r[1].astype(F32)
    fresh_scores = []
    for i in range(8):
        q_i = qf[pl.ds(par * 8 + i, 8, stride=16), :]
        fresh_scores.append([
            jnp.sum(q_i * fresh_k[t * 8:(t + 1) * 8], axis=1, keepdims=True) * scale
            for t in range(i // 4 + 1)])

    wait_all(eo.at[pl.ds(0, nl - 1)], recv.at[S_OWN])
    wait_all(el.at[pl.ds(0, nl - 1)], recv.at[S_EL])
    wait_all(er.at[pl.ds(0, nl - 1)], recv.at[S_E])
    request = lax.broadcasted_iota(jnp.int32, (req, 128), 0)
    owned, logs = [], []
    for k in range(nl // 4):
        o, s = eo[4 * k], el[4 * k]
        for x in range(1, 4):
            o = jnp.maximum(o, eo[4 * k + x])
            s = jnp.maximum(s, el[4 * k + x])
        owned.append(o[0:1] == request)
        logs.append(s)
    laneq = lax.broadcasted_iota(jnp.int32, (req, 128), 1)
    lse_out = jnp.full((req, 128), NEG, F32)
    for i in range(8):
        masked = [jnp.where(owned[k], logs[k][i:i + 1], NEG) for k in range(nl // 4)]
        m = masked[0]
        for k in range(1, nl // 4):
            m = jnp.maximum(m, masked[k])
        m = jnp.max(m, axis=1, keepdims=True)
        weights = [jnp.where(x > 0.5 * NEG, jnp.exp2(x - m), 0.0) for x in masked]
        t = weights[0]
        for k in range(1, nl // 4):
            t = t + weights[k]
        t = jnp.sum(t, axis=1, keepdims=True)
        weights = jnp.concatenate(weights, axis=1).astype(BF16)
        data = er[:, i * slots:(i + 1) * slots, :].reshape(nl * slots, HD)
        o = jnp.dot(weights, data, preferred_element_type=F32) / jnp.maximum(t, 1e-30)
        ff[:, i * 8:(i + 1) * 8, :] = o.reshape(ng, 8, HD)
        lse = jnp.where(t > 0.0, m + jnp.log(jnp.maximum(t, 1e-30)) * LOG2E, NEG)
        lse_out = jnp.where(laneq == i, lse, lse_out)
    fb[...] = ff[...].astype(BF16)
    fl[...] = lse_out.reshape(ng, 8, 128)
    fr[g] = fb[g]
    frl[g] = fl[g]

    def send_f(k):
        gg = lax.rem(g + k, ng)
        copy(fb.at[gg], fr.at[g], S_F, gg, l).start()
        copy(fl.at[gg], frl.at[g], S_FL, gg, l).start()
    each(ng, send_f)

    wait_all(frl.at[pl.ds(0, ng - 1)], recv.at[S_FL])
    wait_all(fr.at[pl.ds(0, ng - 1)], recv.at[S_F])
    data = [fr[gg].astype(F32) for gg in range(ng)]
    logs = [frl[gg] for gg in range(ng)]
    for s in range(steps):
        pieces = []
        for j in range(4):
            i = s * 4 + j
            parts = [(logs[gg][:, i:i + 1], data[gg][i * 8:(i + 1) * 8]) for gg in range(ng)]
            parts += [(fresh_scores[i][t], fresh_v[t * 8:(t + 1) * 8]) for t in range(s + 1)]
            m = parts[0][0]
            for score, unused in parts[1:]:
                m = jnp.maximum(m, score)
            total = jnp.zeros((8, 1), F32)
            o = jnp.zeros((8, HD), F32)
            for score, value in parts:
                w = jnp.exp2(score - m)
                total = total + w
                o = o + w * value
            pieces.append(o / total)
        out[s] = jnp.concatenate(pieces, axis=1).astype(BF16)

    wait_all(wkv_v.at[pl.ds(0, (nl - 1) * kvrows)], send.at[S_KVW])
    wait_all(eo.at[pl.ds(0, nl - 1)], send.at[S_OWN])
    wait_all(rs.at[pl.ds(0, nch - 1)], send.at[S_RS])
    wait_all(frs.at[pl.ds(0, ng - 1)], send.at[S_FRS])
    wait_all(q_all.at[pl.ds(0, 2), 0, pl.ds(0, nl - 1)], send.at[S_G1])
    wait_all(q_all.at[pl.ds(0, 2), 0, pl.ds(0, ny - 1)], send.at[S_G2])
    wait_all(q_all.at[:, pl.ds(0, ny - 1), pl.ds(0, 4)], send.at[S_H1])
    wait_all(q_all.at[:, 0, pl.ds(0, (nl - 1) * ny * 2 // kvh)], send.at[S_H2])
    wait_all(q_all.at[:, :, pl.ds(0, 8)], send.at[S_SIB])
    for kind in range(2):
        for pp in range(2):
            @pl.when((which == kind) & ((l % kvh) * 2 + pp != l))
            def _():
                wait_all(kvown, send.at[S_KEY + kind])
    wait_all(er.at[pl.ds(0, nl - 1)], send.at[S_E])
    wait_all(el.at[pl.ds(0, nl - 1)], send.at[S_EL])
    wait_all(fr.at[pl.ds(0, ng - 1)], send.at[S_F])
    wait_all(frl.at[pl.ds(0, ng - 1)], send.at[S_FL])


def per_device(ng, nl, tokens, query_weight, kv_weight, pages, slot_request, slot_len):
    steps, req, width = tokens.shape
    rows = query_weight.shape[0]
    slots, unused, page, kvwidth = pages.shape
    kvh = kvwidth // HD
    ny = ng // CORES
    hbm = pl.BlockSpec(memory_space=pl.ANY)
    smem = pl.BlockSpec(memory_space=pltpu.SMEM)
    scratch = [
        pltpu.VMEM((steps, req, rows), BF16),
        pltpu.VMEM((rows, 4 * HD), BF16),
        pltpu.VMEM((rows, HD), BF16),
        pltpu.VMEM(pages.shape, BF16),
        pltpu.VMEM((2 * ng, 8, 4 * HD), F32),
        pltpu.VMEM((2 * ng, 8, 4 * HD), F32),
        pltpu.VMEM((steps, req, HD), F32),
        pltpu.VMEM((ng, steps, 8, HD), F32),
        pltpu.VMEM((steps * 8, HD), BF16),
        pltpu.VMEM((2, steps * 8, HD), BF16),
        pltpu.VMEM((kvh, ny, 16, 16, HD), BF16),
        pltpu.VMEM((8, 128), jnp.int32),
        pltpu.VMEM((nl, 8, 128), jnp.int32),
        pltpu.VMEM((16 * slots, HD), F32),
        pltpu.VMEM((nl, 8 * slots, HD), BF16),
        pltpu.VMEM((nl, 8, 128), F32),
        pltpu.VMEM((nl, 8 * slots, HD), BF16),
        pltpu.VMEM((nl, 8, 128), F32),
        pltpu.VMEM((ng, 64, HD), F32),
        pltpu.VMEM((ng, 64, HD), BF16),
        pltpu.VMEM((ng, 8, 128), F32),
        pltpu.VMEM((ng, 64, HD), BF16),
        pltpu.VMEM((ng, 8, 128), F32),
        pltpu.VMEM((128, HD), F32),
        pltpu.SemaphoreType.DMA((15,)),
        pltpu.SemaphoreType.DMA((15,)),
        pltpu.SemaphoreType.DMA((4,)),
    ]
    return pl.pallas_call(
        functools.partial(kernel, ng, nl),
        out_shape=jax.ShapeDtypeStruct((steps, req // ng, 4 * HD), BF16),
        in_specs=[hbm, hbm, hbm, hbm, smem, smem],
        out_specs=pl.BlockSpec(memory_space=pltpu.VMEM),
        scratch_shapes=scratch,
        compiler_params=pltpu.CompilerParams(
            collective_id=0, has_side_effects=True, vmem_limit_bytes=62 * 1024 * 1024),
    )(tokens, query_weight, kv_weight, pages, slot_request, slot_len)


def solution(mesh):
    ng, nl = mesh.shape["group"], mesh.shape["lend"]
    return jax.shard_map(
        functools.partial(per_device, ng, nl),
        mesh=mesh,
        in_specs=(
            P(),
            P("group", "lend"),
            P(("group", "lend"), None),
            P(("group", "lend"), None, None, None),
            P(("group", "lend")),
            P(("group", "lend")),
        ),
        out_specs=P(None, "group", "lend"),
        check_vma=False,
    )
```

```python
import functools

import jax
import jax.numpy as jnp
from jax import lax
from jax.experimental import pallas as pl
from jax.experimental.pallas import tpu as pltpu
from jax.sharding import PartitionSpec as P

HD = 128
CORES = 2
NEG = -1e30
LOG2E = 1.4426950408889634
MESH = pl.DeviceIdType.MESH
F32 = jnp.float32
BF16 = jnp.bfloat16
UNROLL = 16
SPLIT = 3
AHEAD = 8

(S_KVW, S_RS, S_FRS, S_KEY, S_VAL, S_G1, S_G2, S_H1, S_H2, S_SIB,
 S_E, S_F) = range(12)
H_G1, H_H1, H_H2, H_SIB = range(4)
L_TOK, L_WQ, L_KV, L_PAGES = range(4)


def pieces_of(x):
    hi = x.astype(BF16).astype(F32)
    mid = (x - hi).astype(BF16).astype(F32)
    return hi, mid, x - hi - mid


def kernel(ng, nl, tok, wq, kvw, pages, own_s, len_s, out,
           tok_v, wq_v, wkv_v, pages_v, qpart, rs, fpart, frs, kvown, kv_r, q_all,
           slot_o, res, er, ff, fb, fr, qf, q_head,
           send, recv, by_head, local):
    g = lax.axis_index("group")
    l = lax.axis_index("lend")
    y, c = g // CORES, g % CORES
    ny = ng // CORES
    h_own, par = l // 2, l % 2
    kvh = nl // 2
    nch = 2 * ng
    offsets = (2, 7, 1, 4, 3, 6, 5, 0) if kvh == 8 else tuple(range(kvh - 1, -1, -1))
    table = sum(offset * 8 ** i for i, offset in enumerate(offsets))
    turn = 1 - 2 * par

    def head_at(i):
        offset = (table >> (3 * i)) & 7
        nx = nl // 4
        hx = lax.rem(l // 4 + turn * (offset // 2) + nx, nx)
        return hx * 2 + (h_own + offset) % 2

    slots = pages.shape[0]
    page = pages.shape[2]
    steps, req, rows = tok_v.shape
    kvrows = kvw.shape[0]

    def copy(src, dst, which, gg, ll):
        return pltpu.make_async_remote_copy(
            src_ref=src, dst_ref=dst, send_sem=send.at[which], recv_sem=recv.at[which],
            device_id=(gg, ll), device_id_type=MESH)

    def head_copy(block, which, kind, h, gg, ll):
        return pltpu.make_async_remote_copy(
            src_ref=block, dst_ref=block, send_sem=send.at[which], recv_sem=by_head.at[kind, h],
            device_id=(gg, ll), device_id_type=MESH)

    def wait_all(ref, sem):
        pltpu.make_async_copy(ref, ref, sem).wait()

    def each(n, body):
        def step(k, carry):
            body(k)
            return carry
        lax.fori_loop(1, n, step, 0)

    for s in range(steps):
        pltpu.make_async_copy(
            tok.at[s, :, pl.ds(pl.multiple_of(g * rows, 128), rows)], tok_v.at[s], local.at[L_TOK]).start()
    quarter_rows = rows // 4
    for k in range(4):
        part_rows = pl.ds(k * quarter_rows, quarter_rows)
        pltpu.make_async_copy(wq.at[part_rows], wq_v.at[part_rows], local.at[L_WQ]).start()
    c_kv = pltpu.make_async_copy(
        kvw.at[:, pl.ds(pl.multiple_of(l * HD, HD), HD)],
        wkv_v.at[pl.ds(pl.multiple_of(l * kvrows, kvrows), kvrows)], local.at[L_KV])
    c_kv.start()

    barrier = pltpu.get_barrier_semaphore()

    def greet(gg, ll):
        pl.semaphore_signal(barrier, inc=1, device_id=(gg, ll), device_id_type=MESH)

    each(nl, lambda k: greet(g, lax.rem(l + k, nl)))

    def greet_group(k):
        gg = lax.rem(g + k, ng)
        greet(gg, l)
        greet(gg, h_own * 2 + (1 - par))
    each(ng, greet_group)

    def start_pages(k, carry):
        pltpu.make_async_copy(pages.at[pl.ds(k * 2, 2)], pages_v.at[pl.ds(k * 2, 2)], local.at[L_PAGES]).start()
        return carry
    lax.fori_loop(0, slots // 2, start_pages, 0)

    wait_all(tok_v, local.at[L_TOK])
    tokens = tok_v[...].reshape(steps * req, rows)
    wait_all(wq_v, local.at[L_WQ])
    part = jnp.dot(tokens, wq_v[...], preferred_element_type=F32).reshape(steps, ng, 8, 4 * HD)
    upper = lax.broadcasted_iota(jnp.int32, (8, 4 * HD), 0) < 4
    for gg in range(ng):
        first, second = part[0, gg], part[1, gg]
        qpart[2 * gg] = jnp.where(upper, first, pltpu.roll(second, 4, 0))
        qpart[2 * gg + 1] = jnp.where(upper, pltpu.roll(first, 4, 0), second)
    mine = g * 2 + par
    rs[mine] = qpart[mine]

    pl.semaphore_wait(barrier, (nl - 1) + 2 * (ng - 1))

    def send_rs(k):
        idx = lax.rem(mine + k, nch)
        copy(qpart.at[idx], rs.at[mine], S_RS, idx // 2, h_own * 2 + idx % 2).start()
    each(nch, send_rs)

    wait_all(rs.at[pl.ds(0, nch - 1)], recv.at[S_RS])
    blocks = []
    for half in range(2):
        total = rs[half]
        for gg in range(1, ng):
            total = total + rs[2 * gg + half]
        for j in range(4):
            blocks.append(total[:, j * HD:(j + 1) * HD])
    stacked = jnp.concatenate(blocks, axis=0).astype(BF16)
    to = lax.broadcasted_iota(jnp.int32, (64, 64), 0)
    fro = lax.broadcasted_iota(jnp.int32, (64, 64), 1)
    source = ((to // 8) % 2) * 32 + (to % 4) * 8 + ((to // 4) % 2) * 4 + to // 16
    order = jnp.where(fro == source, 1.0, 0.0).astype(BF16)
    chunk = jnp.dot(order, stacked, preferred_element_type=F32).astype(BF16)
    for r4 in range(4):
        q_all[h_own, y, c, r4, par] = chunk[r4 * 16:(r4 + 1) * 16]

    piece1 = q_all.at[h_own, y, c, pl.ds(0, SPLIT), par]
    piece2 = q_all.at[h_own, y, c, pl.ds(SPLIT, 4 - SPLIT), par]

    def send_g2(k):
        copy(piece2, piece2, S_G2, lax.rem(y + k, ny) * CORES + c, l).start()
    each(ny, send_g2)

    def send_g1(k):
        head_copy(piece1, S_G1, H_G1, h_own, g, lax.rem(l + nl - k, nl)).start()
    each(nl, send_g1)

    def send_kv(k):
        ll = lax.rem(l + k, nl)
        copy(kvw.at[:, pl.ds(pl.multiple_of(ll * HD, HD), HD)],
             wkv_v.at[pl.ds(pl.multiple_of(l * kvrows, kvrows), kvrows)], S_KVW, g, ll).start()
    each(nl, send_kv)

    def send_h2(k):
        block = q_all.at[h_own, :, c, pl.ds(SPLIT, 4 - SPLIT), par]
        head_copy(block, S_H2, H_H2, h_own, g, lax.rem(l + nl - k, nl)).start()

    def wait_pair(both, one, sem, h):
        @pl.when(h == h_own)
        def _():
            wait_all(one, sem)

        @pl.when(h != h_own)
        def _():
            wait_all(both, sem)

    wait_all(er.at[pl.ds(0, ny - 1), pl.ds(0, 16 * (4 - SPLIT))], recv.at[S_G2])

    def onward(i):
        h = head_at(i)
        wait_pair(q_all.at[h, 0, 0, pl.ds(0, SPLIT)], q_all.at[h, 0, 0, pl.ds(0, SPLIT), 0], by_head.at[H_G1, h], h)

        def send_h1(k):
            gg = lax.rem(y + k, ny) * CORES + c
            head_copy(q_all.at[h, y, c, pl.ds(0, SPLIT)], S_H1, H_H1, h, gg, l).start()
        each(ny, send_h1)

    ahead = min(AHEAD, kvh)
    onward(0)
    each(nl, send_h2)
    each(ahead, onward)

    lane = lax.broadcasted_iota(jnp.int32, (8, 128), 1)
    quarter = (l % 4) * slots
    owners = jnp.full((8, 128), -1, jnp.int32)
    for p in range(slots):
        owners = jnp.where(lane == quarter + p, own_s[p], owners)
    owners = owners.astype(F32)

    which = l // kvh

    def fresh_parts():
        c_kv.wait()
        wait_all(wkv_v.at[pl.ds(0, (nl - 1) * kvrows)], recv.at[S_KVW])
        fpart[...] = jnp.dot(tokens, wkv_v[...], preferred_element_type=F32).reshape(steps, req, HD)
        frs[g] = fpart[:, pl.ds(pl.multiple_of(g * 8, 8), 8), :]

        def send_frs(k):
            gg = lax.rem(g + k, ng)
            copy(fpart.at[:, pl.ds(pl.multiple_of(gg * 8, 8), 8), :], frs.at[g], S_FRS, gg, l).start()
        each(ng, send_frs)

    def fresh_total():
        wait_all(frs.at[pl.ds(0, ng - 1)], recv.at[S_FRS])
        total = frs[0]
        for gg in range(1, ng):
            total = total + frs[gg]
        kvown[...] = total.reshape(steps * 8, HD).astype(BF16)
        for pp in range(2):
            ll = (l % kvh) * 2 + pp

            @pl.when(ll == l)
            def _():
                kv_r[which] = kvown[...]

            for kind in range(2):
                @pl.when((ll != l) & (which == kind))
                def _():
                    copy(kvown, kv_r.at[kind], S_KEY + kind, g, ll).start()

    def to_sibling(i):
        h = head_at(i)
        wait_all(q_all.at[h, pl.ds(0, ny - 1), 0, pl.ds(0, SPLIT)], by_head.at[H_H1, h])
        wait_pair(q_all.at[h, :, 0, pl.ds(SPLIT, 4 - SPLIT)], q_all.at[h, :, 0, pl.ds(SPLIT, 4 - SPLIT), 0],
                  by_head.at[H_H2, h], h)
        head_copy(q_all.at[h, :, c], S_SIB, H_SIB, h, y * CORES + (1 - c), l).start()

    to_sibling(0)
    wait_all(pages_v, local.at[L_PAGES])

    scale = LOG2E / (HD ** 0.5)
    lane16 = lax.broadcasted_iota(jnp.int32, (16, 128), 1)

    def head(i, carry):
        h = head_at(i)
        columns = pl.ds(pl.multiple_of(h * HD, HD), HD)

        @pl.when(i < kvh - ahead)
        def _():
            onward(i + ahead)

        @pl.when(i < kvh - 1)
        def _():
            to_sibling(i + 1)

        wait_all(q_all.at[h, :, 0], by_head.at[H_SIB, h])
        q_head[...] = q_all[h]

        @pl.when(i == (2 if kvh > 2 else 0))
        def _():
            fresh_parts()

        @pl.when(i == (5 if kvh > 5 else 1))
        def _():
            fresh_total()

        def visit(b, state):
            maxima, sums = state
            block = [b * UNROLL + u for u in range(UNROLL)]
            scores = []
            for p in block:
                r = own_s[p]
                scores.append(lax.dot_general(
                    q_head[r // 16, (r // 8) % 2, r % 4, (r // 4) % 2], pages_v[p, 0, :, columns],
                    (((1,), (1,)), ((), ())), preferred_element_type=F32) * scale)
            valid = [lane16 < len_s[p] for p in block]
            scores = [jnp.where(ok, x, NEG) for ok, x in zip(valid, scores)]
            tops = [jnp.max(x, axis=1, keepdims=True) for x in scores]
            weights = [jnp.where(ok, jnp.exp2(x - m), 0.0) for ok, x, m in zip(valid, scores, tops)]
            totals = [jnp.sum(w, axis=1, keepdims=True) for w in weights]
            outs = [
                jnp.dot(w.astype(BF16), pages_v[p, 1, :, columns], preferred_element_type=F32)
                for w, p in zip(weights, block)]
            for p, o, m, t in zip(block, outs, tops, totals):
                slot_o[pl.ds(p, 16, stride=slots), :] = o / jnp.maximum(t, 1e-30)
                here = lane16 == quarter + p
                maxima = jnp.where(here, m, maxima)
                sums = jnp.where(here, t, sums)
            return maxima, sums

        maxima, sums = lax.fori_loop(
            0, slots // UNROLL, visit,
            (jnp.full((16, 128), NEG, F32), jnp.zeros((16, 128), F32)))
        lse = jnp.where(sums > 0.0, maxima + jnp.log(jnp.maximum(sums, 1e-30)) * LOG2E, NEG)
        for half in range(2):
            ll = 2 * h + half
            res[ll, pl.ds(0, 8 * slots)] = slot_o[pl.ds(half * 8 * slots, 8 * slots), :].astype(BF16)
            hi, mid, lo = pieces_of(lse[half * 8:(half + 1) * 8])
            res[ll, pl.ds(8 * slots, 16)] = jnp.concatenate([hi, mid], axis=0).astype(BF16)
            res[ll, pl.ds(8 * slots + 16, 16)] = jnp.concatenate([lo, owners], axis=0).astype(BF16)

            @pl.when(ll != l)
            def _():
                copy(res.at[ll], er.at[l], S_E, g, ll).start()

            @pl.when(ll == l)
            def _():
                er[l] = res[ll]
        return carry

    lax.fori_loop(0, kvh, head, 0)

    for r4 in range(4):
        for pp in range(2):
            qf[(pp * 4 + r4) * 16:(pp * 4 + r4 + 1) * 16] = q_all[h_own, y, c, r4, pp].astype(F32)

    @pl.when(l != h_own)
    def _():
        wait_all(kv_r.at[0], recv.at[S_KEY])

    @pl.when(l != kvh + h_own)
    def _():
        wait_all(kv_r.at[1], recv.at[S_VAL])

    fresh_k = kv_r[0].astype(F32)
    fresh_v = kv_r[1].astype(F32)
    fresh_scores = []
    for i in range(8):
        q_i = qf[pl.ds(par * 8 + i, 8, stride=16), :]
        fresh_scores.append([
            jnp.sum(q_i * fresh_k[t * 8:(t + 1) * 8], axis=1, keepdims=True) * scale
            for t in range(i // 4 + 1)])

    wait_all(er.at[pl.ds(0, nl - 1)], recv.at[S_E])
    request = lax.broadcasted_iota(jnp.int32, (req, 128), 0)
    owned, logs = [], []
    for k in range(nl // 4):
        o = s = None
        for x in range(4 * k, 4 * k + 4):
            tail = er[x, pl.ds(8 * slots, 32)].astype(F32)
            lse = tail[0:8] + tail[8:16] + tail[16:24]
            o = tail[24:32] if o is None else jnp.maximum(o, tail[24:32])
            s = lse if s is None else jnp.maximum(s, lse)
        owned.append(o[0:1].astype(jnp.int32) == request)
        logs.append(s)
    laneq = lax.broadcasted_iota(jnp.int32, (req, 128), 1)
    lse_out = jnp.full((req, 128), NEG, F32)
    for i in range(8):
        masked = [jnp.where(owned[k], logs[k][i:i + 1], NEG) for k in range(nl // 4)]
        m = masked[0]
        for k in range(1, nl // 4):
            m = jnp.maximum(m, masked[k])
        m = jnp.max(m, axis=1, keepdims=True)
        weights = [jnp.where(x > 0.5 * NEG, jnp.exp2(x - m), 0.0) for x in masked]
        t = weights[0]
        for k in range(1, nl // 4):
            t = t + weights[k]
        t = jnp.sum(t, axis=1, keepdims=True)
        weights = jnp.concatenate(weights, axis=1).astype(BF16)
        data = er[:, i * slots:(i + 1) * slots, :].reshape(nl * slots, HD)
        o = jnp.dot(weights, data, preferred_element_type=F32) / jnp.maximum(t, 1e-30)
        ff[:, i * 8:(i + 1) * 8, :] = o.reshape(ng, 8, HD)
        lse = jnp.where(t > 0.0, m + jnp.log(jnp.maximum(t, 1e-30)) * LOG2E, NEG)
        lse_out = jnp.where(laneq == i, lse, lse_out)
    hi, mid, lo = pieces_of(lse_out)
    for k, piece in enumerate((hi, mid, lo, jnp.zeros_like(lo))):
        ff[:, 64 + 8 * k:72 + 8 * k, :] = piece.reshape(ng, 8, 128)
    fb[...] = ff[...].astype(BF16)
    fr[g] = fb[g]

    def send_f(k):
        gg = lax.rem(g + k, ng)
        copy(fb.at[gg], fr.at[g], S_F, gg, l).start()
    each(ng, send_f)

    wait_all(fr.at[pl.ds(0, ng - 1)], recv.at[S_F])
    data = [fr[gg].astype(F32) for gg in range(ng)]
    logs = [x[64:72] + x[72:80] + x[80:88] for x in data]
    for s in range(steps):
        pieces = []
        for j in range(4):
            i = s * 4 + j
            parts = [(logs[gg][:, i:i + 1], data[gg][i * 8:(i + 1) * 8]) for gg in range(ng)]
            parts += [(fresh_scores[i][t], fresh_v[t * 8:(t + 1) * 8]) for t in range(s + 1)]
            m = parts[0][0]
            for score, unused in parts[1:]:
                m = jnp.maximum(m, score)
            total = jnp.zeros((8, 1), F32)
            o = jnp.zeros((8, HD), F32)
            for score, value in parts:
                w = jnp.exp2(score - m)
                total = total + w
                o = o + w * value
            pieces.append(o / total)
        out[s] = jnp.concatenate(pieces, axis=1).astype(BF16)

    wait_all(wkv_v.at[pl.ds(0, (nl - 1) * kvrows)], send.at[S_KVW])
    wait_all(rs.at[pl.ds(0, nch - 1)], send.at[S_RS])
    wait_all(frs.at[pl.ds(0, ng - 1)], send.at[S_FRS])
    wait_all(er.at[pl.ds(0, nl - 1), pl.ds(0, 16 * SPLIT)], send.at[S_G1])
    wait_all(er.at[pl.ds(0, ny - 1), pl.ds(0, 16 * (4 - SPLIT))], send.at[S_G2])
    wait_all(q_all.at[:, pl.ds(0, ny - 1), 0, pl.ds(0, SPLIT)], send.at[S_H1])
    wait_all(er.at[pl.ds(0, nl - 1), pl.ds(0, 16 * ny * (4 - SPLIT))], send.at[S_H2])
    wait_all(q_all.at[:, :, 0], send.at[S_SIB])
    for kind in range(2):
        for pp in range(2):
            @pl.when((which == kind) & ((l % kvh) * 2 + pp != l))
            def _():
                wait_all(kvown, send.at[S_KEY + kind])
    wait_all(er.at[pl.ds(0, nl - 1)], send.at[S_E])
    wait_all(fr.at[pl.ds(0, ng - 1)], send.at[S_F])


def per_device(ng, nl, tokens, query_weight, kv_weight, pages, slot_request, slot_len):
    steps, req, width = tokens.shape
    rows = query_weight.shape[0]
    slots, unused, page, kvwidth = pages.shape
    kvh = kvwidth // HD
    ny = ng // CORES
    hbm = pl.BlockSpec(memory_space=pl.ANY)
    smem = pl.BlockSpec(memory_space=pltpu.SMEM)
    scratch = [
        pltpu.VMEM((steps, req, rows), BF16),
        pltpu.VMEM((rows, 4 * HD), BF16),
        pltpu.VMEM((rows, HD), BF16),
        pltpu.VMEM(pages.shape, BF16),
        pltpu.VMEM((2 * ng, 8, 4 * HD), F32),
        pltpu.VMEM((2 * ng, 8, 4 * HD), F32),
        pltpu.VMEM((steps, req, HD), F32),
        pltpu.VMEM((ng, steps, 8, HD), F32),
        pltpu.VMEM((steps * 8, HD), BF16),
        pltpu.VMEM((2, steps * 8, HD), BF16),
        pltpu.VMEM((kvh, ny, 2, 4, 2, 16, HD), BF16),
        pltpu.VMEM((16 * slots, HD), F32),
        pltpu.VMEM((nl, 8 * slots + 32, HD), BF16),
        pltpu.VMEM((nl, 8 * slots + 32, HD), BF16),
        pltpu.VMEM((ng, 96, HD), F32),
        pltpu.VMEM((ng, 96, HD), BF16),
        pltpu.VMEM((ng, 96, HD), BF16),
        pltpu.VMEM((128, HD), F32),
        pltpu.VMEM((ny, 2, 4, 2, 16, HD), BF16),
        pltpu.SemaphoreType.DMA((12,)),
        pltpu.SemaphoreType.DMA((12,)),
        pltpu.SemaphoreType.DMA((4, kvh)),
        pltpu.SemaphoreType.DMA((4,)),
    ]
    return pl.pallas_call(
        functools.partial(kernel, ng, nl),
        out_shape=jax.ShapeDtypeStruct((steps, req // ng, 4 * HD), BF16),
        in_specs=[hbm, hbm, hbm, hbm, smem, smem],
        out_specs=pl.BlockSpec(memory_space=pltpu.VMEM),
        scratch_shapes=scratch,
        compiler_params=pltpu.CompilerParams(
            collective_id=0, has_side_effects=True, vmem_limit_bytes=62 * 1024 * 1024),
    )(tokens, query_weight, kv_weight, pages, slot_request, slot_len)


def solution(mesh):
    ng, nl = mesh.shape["group"], mesh.shape["lend"]
    return jax.shard_map(
        functools.partial(per_device, ng, nl),
        mesh=mesh,
        in_specs=(
            P(),
            P("group", "lend"),
            P(("group", "lend"), None),
            P(("group", "lend"), None, None, None),
            P(("group", "lend")),
            P(("group", "lend")),
        ),
        out_specs=P(None, "group", "lend"),
        check_vma=False,
    )
```

```python
import functools

import jax
import jax.numpy as jnp
from jax import lax
from jax.experimental import pallas as pl
from jax.experimental.pallas import tpu as pltpu
from jax.sharding import PartitionSpec as P

HD = 128
CORES = 2
NEG = -1e30
LOG2E = 1.4426950408889634
MESH = pl.DeviceIdType.MESH
F32 = jnp.float32
BF16 = jnp.bfloat16
UNROLL = 32
SPLIT = 3
AHEAD = 8

(S_KVW, S_RS, S_FRS, S_KEY, S_VAL, S_G1, S_G2, S_H1, S_H2, S_SIB,
 S_E, S_F) = range(12)
H_G1, H_H1, H_H2, H_SIB = range(4)
L_TOK, L_WQ, L_KV, L_PAGES = range(4)


def pieces_of(x):
    hi = x.astype(BF16).astype(F32)
    mid = (x - hi).astype(BF16).astype(F32)
    return hi, mid, x - hi - mid


def kernel(ng, nl, tok, wq, kvw, pages, own_s, len_s, out,
           tok_v, wq_v, wkv_v, pages_v, qpart, rs, fpart, frs, kvown, kv_r, q_all,
           slot_o, res, er, ff, fb, fr, qf, q_head,
           send, recv, by_head, local):
    g = lax.axis_index("group")
    l = lax.axis_index("lend")
    y, c = g // CORES, g % CORES
    ny = ng // CORES
    h_own, par = l // 2, l % 2
    kvh = nl // 2
    nch = 2 * ng
    offsets = (2, 7, 1, 4, 3, 6, 5, 0) if kvh == 8 else tuple(range(kvh - 1, -1, -1))
    table = sum(offset * 8 ** i for i, offset in enumerate(offsets))
    turn = 1 - 2 * par

    def head_at(i):
        offset = (table >> (3 * i)) & 7
        nx = nl // 4
        hx = lax.rem(l // 4 + turn * (offset // 2) + nx, nx)
        return hx * 2 + (h_own + offset) % 2

    slots = pages.shape[0]
    page = pages.shape[2]
    steps, req, rows = tok_v.shape
    kvrows = kvw.shape[0]

    def copy(src, dst, which, gg, ll):
        return pltpu.make_async_remote_copy(
            src_ref=src, dst_ref=dst, send_sem=send.at[which], recv_sem=recv.at[which],
            device_id=(gg, ll), device_id_type=MESH)

    def head_copy(block, which, kind, h, gg, ll):
        return pltpu.make_async_remote_copy(
            src_ref=block, dst_ref=block, send_sem=send.at[which], recv_sem=by_head.at[kind, h],
            device_id=(gg, ll), device_id_type=MESH)

    def wait_all(ref, sem):
        pltpu.make_async_copy(ref, ref, sem).wait()

    def each(n, body, far=False):
        def step(k, carry):
            body(1 + lax.rem(k + n // 2 - 2, n - 1) if far else k)
            return carry
        lax.fori_loop(1, n, step, 0)

    for s in range(steps):
        pltpu.make_async_copy(
            tok.at[s, :, pl.ds(pl.multiple_of(g * rows, 128), rows)], tok_v.at[s], local.at[L_TOK]).start()
    quarter_rows = rows // 4
    for k in range(4):
        part_rows = pl.ds(k * quarter_rows, quarter_rows)
        pltpu.make_async_copy(wq.at[part_rows], wq_v.at[part_rows], local.at[L_WQ]).start()
    c_kv = pltpu.make_async_copy(
        kvw.at[:, pl.ds(pl.multiple_of(l * HD, HD), HD)],
        wkv_v.at[pl.ds(pl.multiple_of(l * kvrows, kvrows), kvrows)], local.at[L_KV])
    c_kv.start()

    barrier = pltpu.get_barrier_semaphore()

    def greet(gg, ll):
        pl.semaphore_signal(barrier, inc=1, device_id=(gg, ll), device_id_type=MESH)

    each(nl, lambda k: greet(g, lax.rem(l + k, nl)))

    def greet_group(k):
        gg = lax.rem(g + k, ng)
        greet(gg, l)
        greet(gg, h_own * 2 + (1 - par))
    each(ng, greet_group)

    def start_pages(k, carry):
        pltpu.make_async_copy(pages.at[pl.ds(k * 2, 2)], pages_v.at[pl.ds(k * 2, 2)], local.at[L_PAGES]).start()
        return carry
    lax.fori_loop(0, slots // 2, start_pages, 0)

    wait_all(tok_v, local.at[L_TOK])
    tokens = tok_v[...].reshape(steps * req, rows)
    wait_all(wq_v, local.at[L_WQ])
    part = jnp.dot(tokens, wq_v[...], preferred_element_type=F32).reshape(steps, ng, 8, 4 * HD)
    upper = lax.broadcasted_iota(jnp.int32, (8, 4 * HD), 0) < 4
    for gg in range(ng):
        first, second = part[0, gg], part[1, gg]
        qpart[2 * gg] = jnp.where(upper, first, pltpu.roll(second, 4, 0))
        qpart[2 * gg + 1] = jnp.where(upper, pltpu.roll(first, 4, 0), second)
    mine = g * 2 + par
    rs[mine] = qpart[mine]

    pl.semaphore_wait(barrier, (nl - 1) + 2 * (ng - 1))

    def send_rs(k):
        idx = lax.rem(mine + k, nch)
        copy(qpart.at[idx], rs.at[mine], S_RS, idx // 2, h_own * 2 + idx % 2).start()
    each(nch, send_rs, far=True)

    wait_all(rs.at[pl.ds(0, nch - 1)], recv.at[S_RS])
    blocks = []
    for half in range(2):
        total = rs[half]
        for gg in range(1, ng):
            total = total + rs[2 * gg + half]
        for j in range(4):
            blocks.append(total[:, j * HD:(j + 1) * HD])
    stacked = jnp.concatenate(blocks, axis=0).astype(BF16)
    to = lax.broadcasted_iota(jnp.int32, (64, 64), 0)
    fro = lax.broadcasted_iota(jnp.int32, (64, 64), 1)
    source = ((to // 8) % 2) * 32 + (to % 4) * 8 + ((to // 4) % 2) * 4 + to // 16
    order = jnp.where(fro == source, 1.0, 0.0).astype(BF16)
    chunk = jnp.dot(order, stacked, preferred_element_type=F32).astype(BF16)
    for r4 in range(4):
        q_all[h_own, y, c, par, r4] = chunk[r4 * 16:(r4 + 1) * 16]

    piece1 = q_all.at[h_own, y, c, par, pl.ds(0, SPLIT)]
    piece2 = q_all.at[h_own, y, c, par, pl.ds(SPLIT, 4 - SPLIT)]

    def send_g2(k):
        copy(piece2, piece2, S_G2, lax.rem(y + k, ny) * CORES + c, l).start()
    each(ny, send_g2)

    def send_g1(k):
        head_copy(piece1, S_G1, H_G1, h_own, g, lax.rem(l + nl - k, nl)).start()
    each(nl, send_g1, far=True)

    def send_h2(k):
        block = q_all.at[h_own, :, c, par, pl.ds(SPLIT, 4 - SPLIT)]
        head_copy(block, S_H2, H_H2, h_own, g, lax.rem(l + nl - k, nl)).start()

    def wait_pair(both, one, sem, h):
        @pl.when(h == h_own)
        def _():
            wait_all(one, sem)

        @pl.when(h != h_own)
        def _():
            wait_all(both, sem)

    wait_all(er.at[pl.ds(0, ny - 1), pl.ds(0, 16 * (4 - SPLIT))], recv.at[S_G2])

    def onward(i):
        h = head_at(i)
        wait_pair(q_all.at[h, 0, 0, :, pl.ds(0, SPLIT)], q_all.at[h, 0, 0, 0, pl.ds(0, SPLIT)], by_head.at[H_G1, h], h)

        def send_h1(k):
            gg = lax.rem(y + k, ny) * CORES + c
            head_copy(q_all.at[h, y, c, :, pl.ds(0, SPLIT)], S_H1, H_H1, h, gg, l).start()
        each(ny, send_h1)

    ahead = min(AHEAD, kvh)
    onward(0)
    each(nl, send_h2)
    each(ahead, onward)

    def send_kv(k):
        ll = lax.rem(l + k, nl)
        copy(kvw.at[:, pl.ds(pl.multiple_of(ll * HD, HD), HD)],
             wkv_v.at[pl.ds(pl.multiple_of(l * kvrows, kvrows), kvrows)], S_KVW, g, ll).start()
    each(nl, send_kv)

    lane = lax.broadcasted_iota(jnp.int32, (8, 128), 1)
    owners = jnp.full((8, 128), -1, jnp.int32)
    for p in range(slots):
        owners = jnp.where(lane == p, own_s[p], owners)
    owners = owners.astype(F32)

    which = l // kvh

    def fresh_parts():
        c_kv.wait()
        wait_all(wkv_v.at[pl.ds(0, (nl - 1) * kvrows)], recv.at[S_KVW])
        fpart[...] = jnp.dot(tokens, wkv_v[...], preferred_element_type=F32).reshape(steps, req, HD)
        frs[g] = fpart[:, pl.ds(pl.multiple_of(g * 8, 8), 8), :]

        def send_frs(k):
            gg = lax.rem(g + k, ng)
            copy(fpart.at[:, pl.ds(pl.multiple_of(gg * 8, 8), 8), :], frs.at[g], S_FRS, gg, l).start()
        each(ng, send_frs)

    def fresh_total():
        wait_all(frs.at[pl.ds(0, ng - 1)], recv.at[S_FRS])
        total = frs[0]
        for gg in range(1, ng):
            total = total + frs[gg]
        kvown[...] = total.reshape(steps * 8, HD).astype(BF16)
        for pp in range(2):
            ll = (l % kvh) * 2 + pp

            @pl.when(ll == l)
            def _():
                kv_r[which] = kvown[...]

            for kind in range(2):
                @pl.when((ll != l) & (which == kind))
                def _():
                    copy(kvown, kv_r.at[kind], S_KEY + kind, g, ll).start()

    def to_sibling(i):
        h = head_at(i)
        wait_all(q_all.at[h, pl.ds(0, ny - 1), 0, :, pl.ds(0, SPLIT)], by_head.at[H_H1, h])
        wait_pair(q_all.at[h, :, 0, :, pl.ds(SPLIT, 4 - SPLIT)], q_all.at[h, :, 0, 0, pl.ds(SPLIT, 4 - SPLIT)],
                  by_head.at[H_H2, h], h)
        head_copy(q_all.at[h, :, c], S_SIB, H_SIB, h, y * CORES + (1 - c), l).start()

    to_sibling(0)
    wait_all(pages_v, local.at[L_PAGES])

    scale = LOG2E / (HD ** 0.5)
    lane16 = lax.broadcasted_iota(jnp.int32, (16, 128), 1)

    def head(i, carry):
        h = head_at(i)
        columns = pl.ds(pl.multiple_of(h * HD, HD), HD)

        @pl.when(i < kvh - ahead)
        def _():
            onward(i + ahead)

        @pl.when(i < kvh - 1)
        def _():
            to_sibling(i + 1)

        wait_all(q_all.at[h, :, 0], by_head.at[H_SIB, h])
        q_head[...] = q_all[h]

        @pl.when(i == (2 if kvh > 2 else 0))
        def _():
            fresh_parts()

        @pl.when(i == (5 if kvh > 5 else 1))
        def _():
            fresh_total()

        def visit(b, state):
            maxima, sums = state
            block = [b * UNROLL + u for u in range(UNROLL)]
            scores = []
            for p in block:
                r = own_s[p]
                scores.append(lax.dot_general(
                    q_head[r // 16, (r // 8) % 2, (r // 4) % 2, r % 4], pages_v[p, 0, :, columns],
                    (((1,), (1,)), ((), ())), preferred_element_type=F32) * scale)
            valid = [lane16 < len_s[p] for p in block]
            scores = [jnp.where(ok, x, NEG) for ok, x in zip(valid, scores)]
            tops = [jnp.max(x, axis=1, keepdims=True) for x in scores]
            weights = [jnp.where(ok, jnp.exp2(x - m), 0.0) for ok, x, m in zip(valid, scores, tops)]
            totals = [jnp.sum(w, axis=1, keepdims=True) for w in weights]
            outs = [
                jnp.dot(w.astype(BF16), pages_v[p, 1, :, columns], preferred_element_type=F32)
                for w, p in zip(weights, block)]
            for p, o, m, t in zip(block, outs, tops, totals):
                slot_o[pl.ds(p, 16, stride=slots), :] = o / jnp.maximum(t, 1e-30)
                here = lane16 == p
                maxima = jnp.where(here, m, maxima)
                sums = jnp.where(here, t, sums)
            return maxima, sums

        maxima, sums = lax.fori_loop(
            0, slots // UNROLL, visit,
            (jnp.full((16, 128), NEG, F32), jnp.zeros((16, 128), F32)))
        lse = jnp.where(sums > 0.0, maxima + jnp.log(jnp.maximum(sums, 1e-30)) * LOG2E, NEG)
        for half in range(2):
            ll = 2 * h + half
            res[ll, pl.ds(0, 8 * slots)] = slot_o[pl.ds(half * 8 * slots, 8 * slots), :].astype(BF16)
            hi, mid, lo = pieces_of(lse[half * 8:(half + 1) * 8])
            tail = hi
            for k, piece in enumerate((mid, lo, owners), 1):
                tail = jnp.where(lane < k * slots, tail, pltpu.roll(piece, k * slots, 1))
            res[ll, pl.ds(8 * slots, 16)] = jnp.concatenate([tail, tail], axis=0).astype(BF16)

            @pl.when(ll != l)
            def _():
                copy(res.at[ll], er.at[l], S_E, g, ll).start()

            @pl.when(ll == l)
            def _():
                er[l] = res[ll]
        return carry

    lax.fori_loop(0, kvh, head, 0)

    for r4 in range(4):
        for pp in range(2):
            qf[(pp * 4 + r4) * 16:(pp * 4 + r4 + 1) * 16] = q_all[h_own, y, c, pp, r4].astype(F32)

    @pl.when(l != h_own)
    def _():
        wait_all(kv_r.at[0], recv.at[S_KEY])

    @pl.when(l != kvh + h_own)
    def _():
        wait_all(kv_r.at[1], recv.at[S_VAL])

    fresh_k = kv_r[0].astype(F32)
    fresh_v = kv_r[1].astype(F32)
    fresh_scores = []
    for i in range(8):
        q_i = qf[pl.ds(par * 8 + i, 8, stride=16), :]
        fresh_scores.append([
            jnp.sum(q_i * fresh_k[t * 8:(t + 1) * 8], axis=1, keepdims=True) * scale
            for t in range(i // 4 + 1)])

    wait_all(er.at[pl.ds(0, nl - 1)], recv.at[S_E])
    request = lax.broadcasted_iota(jnp.int32, (req, 128), 0)
    owned, logs = [], []
    for k in range(nl // 4):
        o = s = None
        for q in range(4):
            tail = er[4 * k + q, pl.ds(8 * slots, 16)].astype(F32)[0:8]
            lse = tail + pltpu.roll(tail, 3 * slots, 1) + pltpu.roll(tail, 2 * slots, 1)
            owner = pltpu.roll(tail, (q + 1) * slots % 128, 1) if q < 3 else tail
            lse = pltpu.roll(lse, q * slots, 1) if q else lse
            o = owner if o is None else jnp.where(lane < q * slots, o, owner)
            s = lse if s is None else jnp.where(lane < q * slots, s, lse)
        owned.append(o[0:1].astype(jnp.int32) == request)
        logs.append(s)
    laneq = lax.broadcasted_iota(jnp.int32, (req, 128), 1)
    lse_out = jnp.full((req, 128), NEG, F32)
    for i in range(8):
        masked = [jnp.where(owned[k], logs[k][i:i + 1], NEG) for k in range(nl // 4)]
        m = masked[0]
        for k in range(1, nl // 4):
            m = jnp.maximum(m, masked[k])
        m = jnp.max(m, axis=1, keepdims=True)
        weights = [jnp.where(x > 0.5 * NEG, jnp.exp2(x - m), 0.0) for x in masked]
        t = weights[0]
        for k in range(1, nl // 4):
            t = t + weights[k]
        t = jnp.sum(t, axis=1, keepdims=True)
        weights = jnp.concatenate(weights, axis=1).astype(BF16)
        data = er[:, i * slots:(i + 1) * slots, :].reshape(nl * slots, HD)
        o = jnp.dot(weights, data, preferred_element_type=F32) / jnp.maximum(t, 1e-30)
        ff[:, i * 8:(i + 1) * 8, :] = o.reshape(ng, 8, HD)
        lse = jnp.where(t > 0.0, m + jnp.log(jnp.maximum(t, 1e-30)) * LOG2E, NEG)
        lse_out = jnp.where(laneq == i, lse, lse_out)
    hi, mid, lo = pieces_of(lse_out)
    for k, piece in enumerate((hi, mid, lo, jnp.zeros_like(lo))):
        ff[:, 64 + 8 * k:72 + 8 * k, :] = piece.reshape(ng, 8, 128)
    fb[...] = ff[...].astype(BF16)
    fr[g] = fb[g]

    def send_f(k):
        gg = lax.rem(g + k, ng)
        copy(fb.at[gg], fr.at[g], S_F, gg, l).start()
    each(ng, send_f, far=True)

    wait_all(fr.at[pl.ds(0, ng - 1)], recv.at[S_F])
    data = [fr[gg].astype(F32) for gg in range(ng)]
    logs = [x[64:72] + x[72:80] + x[80:88] for x in data]
    for s in range(steps):
        pieces = []
        for j in range(4):
            i = s * 4 + j
            parts = [(logs[gg][:, i:i + 1], data[gg][i * 8:(i + 1) * 8]) for gg in range(ng)]
            parts += [(fresh_scores[i][t], fresh_v[t * 8:(t + 1) * 8]) for t in range(s + 1)]
            m = parts[0][0]
            for score, unused in parts[1:]:
                m = jnp.maximum(m, score)
            total = jnp.zeros((8, 1), F32)
            o = jnp.zeros((8, HD), F32)
            for score, value in parts:
                w = jnp.exp2(score - m)
                total = total + w
                o = o + w * value
            pieces.append(o / total)
        out[s] = jnp.concatenate(pieces, axis=1).astype(BF16)

    wait_all(wkv_v.at[pl.ds(0, (nl - 1) * kvrows)], send.at[S_KVW])
    wait_all(rs.at[pl.ds(0, nch - 1)], send.at[S_RS])
    wait_all(frs.at[pl.ds(0, ng - 1)], send.at[S_FRS])
    wait_all(er.at[pl.ds(0, nl - 1), pl.ds(0, 16 * SPLIT)], send.at[S_G1])
    wait_all(er.at[pl.ds(0, ny - 1), pl.ds(0, 16 * (4 - SPLIT))], send.at[S_G2])
    wait_all(q_all.at[:, pl.ds(0, ny - 1), 0, :, pl.ds(0, SPLIT)], send.at[S_H1])
    wait_all(er.at[pl.ds(0, nl - 1), pl.ds(0, 16 * ny * (4 - SPLIT))], send.at[S_H2])
    wait_all(q_all.at[:, :, 0], send.at[S_SIB])
    for kind in range(2):
        for pp in range(2):
            @pl.when((which == kind) & ((l % kvh) * 2 + pp != l))
            def _():
                wait_all(kvown, send.at[S_KEY + kind])
    wait_all(er.at[pl.ds(0, nl - 1)], send.at[S_E])
    wait_all(fr.at[pl.ds(0, ng - 1)], send.at[S_F])


def per_device(ng, nl, tokens, query_weight, kv_weight, pages, slot_request, slot_len):
    steps, req, width = tokens.shape
    rows = query_weight.shape[0]
    slots, unused, page, kvwidth = pages.shape
    kvh = kvwidth // HD
    ny = ng // CORES
    hbm = pl.BlockSpec(memory_space=pl.ANY)
    smem = pl.BlockSpec(memory_space=pltpu.SMEM)
    scratch = [
        pltpu.VMEM((steps, req, rows), BF16),
        pltpu.VMEM((rows, 4 * HD), BF16),
        pltpu.VMEM((rows, HD), BF16),
        pltpu.VMEM(pages.shape, BF16),
        pltpu.VMEM((2 * ng, 8, 4 * HD), F32),
        pltpu.VMEM((2 * ng, 8, 4 * HD), F32),
        pltpu.VMEM((steps, req, HD), F32),
        pltpu.VMEM((ng, steps, 8, HD), F32),
        pltpu.VMEM((steps * 8, HD), BF16),
        pltpu.VMEM((2, steps * 8, HD), BF16),
        pltpu.VMEM((kvh, ny, 2, 2, 4, 16, HD), BF16),
        pltpu.VMEM((16 * slots, HD), F32),
        pltpu.VMEM((nl, 8 * slots + 16, HD), BF16),
        pltpu.VMEM((nl, 8 * slots + 16, HD), BF16),
        pltpu.VMEM((ng, 96, HD), F32),
        pltpu.VMEM((ng, 96, HD), BF16),
        pltpu.VMEM((ng, 96, HD), BF16),
        pltpu.VMEM((128, HD), F32),
        pltpu.VMEM((ny, 2, 2, 4, 16, HD), BF16),
        pltpu.SemaphoreType.DMA((12,)),
        pltpu.SemaphoreType.DMA((12,)),
        pltpu.SemaphoreType.DMA((4, kvh)),
        pltpu.SemaphoreType.DMA((4,)),
    ]
    return pl.pallas_call(
        functools.partial(kernel, ng, nl),
        out_shape=jax.ShapeDtypeStruct((steps, req // ng, 4 * HD), BF16),
        in_specs=[hbm, hbm, hbm, hbm, smem, smem],
        out_specs=pl.BlockSpec(memory_space=pltpu.VMEM),
        scratch_shapes=scratch,
        compiler_params=pltpu.CompilerParams(
            collective_id=0, has_side_effects=True, vmem_limit_bytes=62 * 1024 * 1024),
    )(tokens, query_weight, kv_weight, pages, slot_request, slot_len)


def solution(mesh):
    ng, nl = mesh.shape["group"], mesh.shape["lend"]
    return jax.shard_map(
        functools.partial(per_device, ng, nl),
        mesh=mesh,
        in_specs=(
            P(),
            P("group", "lend"),
            P(("group", "lend"), None),
            P(("group", "lend"), None, None, None),
            P(("group", "lend")),
            P(("group", "lend")),
        ),
        out_specs=P(None, "group", "lend"),
        check_vma=False,
    )
```

```python
import functools

import jax
import jax.numpy as jnp
from jax import lax
from jax.experimental import pallas as pl
from jax.experimental.pallas import tpu as pltpu
from jax.sharding import PartitionSpec as P

HD = 128
CORES = 2
NEG = -1e30
LOG2E = 1.4426950408889634
MESH = pl.DeviceIdType.MESH
F32 = jnp.float32
BF16 = jnp.bfloat16
UNROLL = 32
SPLIT = 3
AHEAD = 8

(S_KVW, S_RS, S_FRS, S_KEY, S_VAL, S_G1, S_G2, S_H1, S_H2, S_SIB,
 S_E, S_F) = range(12)
H_G1, H_H1, H_H2, H_SIB = range(4)
L_TOK, L_WQ, L_KV, L_PAGES = range(4)


def pieces_of(x):
    hi = x.astype(BF16).astype(F32)
    mid = (x - hi).astype(BF16).astype(F32)
    return hi, mid, x - hi - mid


def kernel(ng, nl, tok, wq, kvw, pages, own_s, len_s, out,
           tok_v, wq_v, wkv_v, pages_v, qpart, rs, fpart, frs, kvown, kv_r, q_all,
           slot_o, res, er, ff, fb, fr, qf, q_head,
           send, recv, by_head, local):
    g = lax.axis_index("group")
    l = lax.axis_index("lend")
    y, c = g // CORES, g % CORES
    ny = ng // CORES
    h_own, par = l // 2, l % 2
    kvh = nl // 2
    nch = 2 * ng
    offsets = (2, 7, 1, 4, 3, 6, 5, 0) if kvh == 8 else tuple(range(kvh - 1, -1, -1))
    table = sum(offset * 8 ** i for i, offset in enumerate(offsets))
    turn = 1 - 2 * par

    def head_at(i):
        offset = (table >> (3 * i)) & 7
        nx = nl // 4
        hx = lax.rem(l // 4 + turn * (offset // 2) + nx, nx)
        return hx * 2 + (h_own + offset) % 2

    slots = pages.shape[0]
    page = pages.shape[2]
    steps, req, rows = tok_v.shape
    kvrows = kvw.shape[0]

    def copy(src, dst, which, gg, ll):
        return pltpu.make_async_remote_copy(
            src_ref=src, dst_ref=dst, send_sem=send.at[which], recv_sem=recv.at[which],
            device_id=(gg, ll), device_id_type=MESH)

    def head_copy(block, which, kind, h, gg, ll):
        return pltpu.make_async_remote_copy(
            src_ref=block, dst_ref=block, send_sem=send.at[which], recv_sem=by_head.at[kind, h],
            device_id=(gg, ll), device_id_type=MESH)

    def wait_all(ref, sem):
        pltpu.make_async_copy(ref, ref, sem).wait()

    def each(n, body, far=False):
        def step(k, carry):
            body(1 + lax.rem(k + n // 2 - 2, n - 1) if far else k)
            return carry
        lax.fori_loop(1, n, step, 0)

    for s in range(steps):
        pltpu.make_async_copy(
            tok.at[s, :, pl.ds(pl.multiple_of(g * rows, 128), rows)], tok_v.at[s], local.at[L_TOK]).start()
    quarter_rows = rows // 4
    for k in range(4):
        part_rows = pl.ds(k * quarter_rows, quarter_rows)
        pltpu.make_async_copy(wq.at[part_rows], wq_v.at[part_rows], local.at[L_WQ]).start()
    c_kv = pltpu.make_async_copy(
        kvw.at[:, pl.ds(pl.multiple_of(l * HD, HD), HD)],
        wkv_v.at[pl.ds(pl.multiple_of(l * kvrows, kvrows), kvrows)], local.at[L_KV])
    c_kv.start()

    barrier = pltpu.get_barrier_semaphore()

    def greet(gg, ll):
        pl.semaphore_signal(barrier, inc=1, device_id=(gg, ll), device_id_type=MESH)

    each(nl, lambda k: greet(g, lax.rem(l + k, nl)))

    def greet_group(k):
        gg = lax.rem(g + k, ng)
        greet(gg, l)
        greet(gg, h_own * 2 + (1 - par))
    each(ng, greet_group)

    def start_pages(k, carry):
        pltpu.make_async_copy(pages.at[pl.ds(k * 2, 2)], pages_v.at[pl.ds(k * 2, 2)], local.at[L_PAGES]).start()
        return carry
    lax.fori_loop(0, slots // 2, start_pages, 0)

    wait_all(tok_v, local.at[L_TOK])
    tokens = tok_v[...].reshape(steps * req, rows)
    wait_all(wq_v, local.at[L_WQ])
    part = jnp.dot(tokens, wq_v[...], preferred_element_type=F32).reshape(steps, ng, 8, 4 * HD)
    upper = lax.broadcasted_iota(jnp.int32, (8, 4 * HD), 0) < 4
    for gg in range(ng):
        first, second = part[0, gg], part[1, gg]
        qpart[2 * gg] = jnp.where(upper, first, pltpu.roll(second, 4, 0))
        qpart[2 * gg + 1] = jnp.where(upper, pltpu.roll(first, 4, 0), second)
    mine = g * 2 + par
    rs[mine] = qpart[mine]

    pl.semaphore_wait(barrier, (nl - 1) + 2 * (ng - 1))

    def send_rs(k):
        idx = lax.rem(mine + k, nch)
        copy(qpart.at[idx], rs.at[mine], S_RS, idx // 2, h_own * 2 + idx % 2).start()
    each(nch, send_rs, far=True)

    wait_all(rs.at[pl.ds(0, nch - 1)], recv.at[S_RS])
    blocks = []
    for half in range(2):
        total = rs[half]
        for gg in range(1, ng):
            total = total + rs[2 * gg + half]
        for j in range(4):
            blocks.append(total[:, j * HD:(j + 1) * HD])
    stacked = jnp.concatenate(blocks, axis=0).astype(BF16)
    to = lax.broadcasted_iota(jnp.int32, (64, 64), 0)
    fro = lax.broadcasted_iota(jnp.int32, (64, 64), 1)
    source = ((to // 8) % 2) * 32 + (to % 4) * 8 + ((to // 4) % 2) * 4 + to // 16
    order = jnp.where(fro == source, 1.0, 0.0).astype(BF16)
    chunk = jnp.dot(order, stacked, preferred_element_type=F32).astype(BF16)
    for r4 in range(4):
        q_all[h_own, y, c, par, r4] = chunk[r4 * 16:(r4 + 1) * 16]

    piece1 = q_all.at[h_own, y, c, par, pl.ds(0, SPLIT)]
    piece2 = q_all.at[h_own, y, c, par, pl.ds(SPLIT, 4 - SPLIT)]

    def send_g2(k):
        copy(piece2, piece2, S_G2, lax.rem(y + k, ny) * CORES + c, l).start()
    each(ny, send_g2, far=True)

    def send_g1(k):
        head_copy(piece1, S_G1, H_G1, h_own, g, lax.rem(l + nl - k, nl)).start()
    each(nl, send_g1, far=True)

    def send_h2(k):
        block = q_all.at[h_own, :, c, par, pl.ds(SPLIT, 4 - SPLIT)]
        head_copy(block, S_H2, H_H2, h_own, g, lax.rem(l + nl - k, nl)).start()

    def wait_pair(both, one, sem, h):
        @pl.when(h == h_own)
        def _():
            wait_all(one, sem)

        @pl.when(h != h_own)
        def _():
            wait_all(both, sem)

    wait_all(er.at[pl.ds(0, ny - 1), pl.ds(0, 16 * (4 - SPLIT))], recv.at[S_G2])

    def onward(i):
        h = head_at(i)
        wait_pair(q_all.at[h, 0, 0, :, pl.ds(0, SPLIT)], q_all.at[h, 0, 0, 0, pl.ds(0, SPLIT)], by_head.at[H_G1, h], h)

        def send_h1(k):
            gg = lax.rem(y + k, ny) * CORES + c
            head_copy(q_all.at[h, y, c, :, pl.ds(0, SPLIT)], S_H1, H_H1, h, gg, l).start()
        each(ny, send_h1, far=True)

    ahead = min(AHEAD, kvh)
    onward(0)
    each(nl, send_h2)
    each(ahead, onward)

    def send_kv(k):
        ll = lax.rem(l + k, nl)
        copy(kvw.at[:, pl.ds(pl.multiple_of(ll * HD, HD), HD)],
             wkv_v.at[pl.ds(pl.multiple_of(l * kvrows, kvrows), kvrows)], S_KVW, g, ll).start()
    each(nl, send_kv)

    lane = lax.broadcasted_iota(jnp.int32, (8, 128), 1)
    owners = jnp.full((8, 128), -1, jnp.int32)
    for p in range(slots):
        owners = jnp.where(lane == p, own_s[p], owners)
    owners = owners.astype(F32)

    which = l // kvh

    def fresh_parts():
        c_kv.wait()
        wait_all(wkv_v.at[pl.ds(0, (nl - 1) * kvrows)], recv.at[S_KVW])
        fpart[...] = jnp.dot(tokens, wkv_v[...], preferred_element_type=F32).reshape(steps, req, HD)
        frs[g] = fpart[:, pl.ds(pl.multiple_of(g * 8, 8), 8), :]

        def send_frs(k):
            gg = lax.rem(g + k, ng)
            copy(fpart.at[:, pl.ds(pl.multiple_of(gg * 8, 8), 8), :], frs.at[g], S_FRS, gg, l).start()
        each(ng, send_frs)

    def fresh_total():
        wait_all(frs.at[pl.ds(0, ng - 1)], recv.at[S_FRS])
        total = frs[0]
        for gg in range(1, ng):
            total = total + frs[gg]
        kvown[...] = total.reshape(steps * 8, HD).astype(BF16)
        for pp in range(2):
            ll = (l % kvh) * 2 + pp

            @pl.when(ll == l)
            def _():
                kv_r[which] = kvown[...]

            for kind in range(2):
                @pl.when((ll != l) & (which == kind))
                def _():
                    copy(kvown, kv_r.at[kind], S_KEY + kind, g, ll).start()

    def to_sibling(i):
        h = head_at(i)
        wait_all(q_all.at[h, pl.ds(0, ny - 1), 0, :, pl.ds(0, SPLIT)], by_head.at[H_H1, h])
        wait_pair(q_all.at[h, :, 0, :, pl.ds(SPLIT, 4 - SPLIT)], q_all.at[h, :, 0, 0, pl.ds(SPLIT, 4 - SPLIT)],
                  by_head.at[H_H2, h], h)
        head_copy(q_all.at[h, :, c], S_SIB, H_SIB, h, y * CORES + (1 - c), l).start()

    to_sibling(0)
    wait_all(pages_v, local.at[L_PAGES])

    scale = LOG2E / (HD ** 0.5)
    lane16 = lax.broadcasted_iota(jnp.int32, (16, 128), 1)

    def head(i, carry):
        h = head_at(i)
        columns = pl.ds(pl.multiple_of(h * HD, HD), HD)

        @pl.when(i < kvh - ahead)
        def _():
            onward(i + ahead)

        @pl.when(i < kvh - 1)
        def _():
            to_sibling(i + 1)

        wait_all(q_all.at[h, :, 0], by_head.at[H_SIB, h])
        q_head[...] = q_all[h]

        @pl.when(i == (3 if kvh > 2 else 0))
        def _():
            fresh_parts()

        @pl.when(i == (6 if kvh > 5 else 1))
        def _():
            fresh_total()

        def visit(b, state):
            maxima, sums = state
            block = [b * UNROLL + u for u in range(UNROLL)]
            scores = []
            for p in block:
                r = own_s[p]
                scores.append(lax.dot_general(
                    q_head[r // 16, (r // 8) % 2, (r // 4) % 2, r % 4], pages_v[p, 0, :, columns],
                    (((1,), (1,)), ((), ())), preferred_element_type=F32) * scale)
            valid = [lane16 < len_s[p] for p in block]
            scores = [jnp.where(ok, x, NEG) for ok, x in zip(valid, scores)]
            tops = [jnp.max(x, axis=1, keepdims=True) for x in scores]
            weights = [jnp.where(ok, jnp.exp2(x - m), 0.0) for ok, x, m in zip(valid, scores, tops)]
            totals = [jnp.sum(w, axis=1, keepdims=True) for w in weights]
            outs = [
                jnp.dot(w.astype(BF16), pages_v[p, 1, :, columns], preferred_element_type=F32)
                for w, p in zip(weights, block)]
            for p, o, m, t in zip(block, outs, tops, totals):
                slot_o[pl.ds(p, 16, stride=slots), :] = o / jnp.maximum(t, 1e-30)
                here = lane16 == p
                maxima = jnp.where(here, m, maxima)
                sums = jnp.where(here, t, sums)
            return maxima, sums

        maxima, sums = lax.fori_loop(
            0, slots // UNROLL, visit,
            (jnp.full((16, 128), NEG, F32), jnp.zeros((16, 128), F32)))
        lse = jnp.where(sums > 0.0, maxima + jnp.log(jnp.maximum(sums, 1e-30)) * LOG2E, NEG)
        for half in range(2):
            ll = 2 * h + half
            res[ll, pl.ds(0, 8 * slots)] = slot_o[pl.ds(half * 8 * slots, 8 * slots), :].astype(BF16)
            hi, mid, lo = pieces_of(lse[half * 8:(half + 1) * 8])
            tail = hi
            for k, piece in enumerate((mid, lo, owners), 1):
                tail = jnp.where(lane < k * slots, tail, pltpu.roll(piece, k * slots, 1))
            res[ll, pl.ds(8 * slots, 16)] = jnp.concatenate([tail, tail], axis=0).astype(BF16)

            @pl.when(ll != l)
            def _():
                copy(res.at[ll], er.at[l], S_E, g, ll).start()

            @pl.when(ll == l)
            def _():
                er[l] = res[ll]
        return carry

    lax.fori_loop(0, kvh, head, 0)

    for r4 in range(4):
        for pp in range(2):
            qf[(pp * 4 + r4) * 16:(pp * 4 + r4 + 1) * 16] = q_all[h_own, y, c, pp, r4].astype(F32)

    @pl.when(l != h_own)
    def _():
        wait_all(kv_r.at[0], recv.at[S_KEY])

    @pl.when(l != kvh + h_own)
    def _():
        wait_all(kv_r.at[1], recv.at[S_VAL])

    fresh_k = kv_r[0].astype(F32)
    fresh_v = kv_r[1].astype(F32)
    fresh_scores = []
    for i in range(8):
        q_i = qf[pl.ds(par * 8 + i, 8, stride=16), :]
        fresh_scores.append([
            jnp.sum(q_i * fresh_k[t * 8:(t + 1) * 8], axis=1, keepdims=True) * scale
            for t in range(i // 4 + 1)])

    wait_all(er.at[pl.ds(0, nl - 1)], recv.at[S_E])
    request = lax.broadcasted_iota(jnp.int32, (req, 128), 0)
    owned, logs = [], []
    for k in range(nl // 4):
        o = s = None
        for q in range(4):
            tail = er[4 * k + q, pl.ds(8 * slots, 16)].astype(F32)[0:8]
            lse = tail + pltpu.roll(tail, 3 * slots, 1) + pltpu.roll(tail, 2 * slots, 1)
            owner = pltpu.roll(tail, (q + 1) * slots % 128, 1) if q < 3 else tail
            lse = pltpu.roll(lse, q * slots, 1) if q else lse
            o = owner if o is None else jnp.where(lane < q * slots, o, owner)
            s = lse if s is None else jnp.where(lane < q * slots, s, lse)
        owned.append(o[0:1].astype(jnp.int32) == request)
        logs.append(s)
    laneq = lax.broadcasted_iota(jnp.int32, (req, 128), 1)
    lse_out = jnp.full((req, 128), NEG, F32)
    for i in range(8):
        masked = [jnp.where(owned[k], logs[k][i:i + 1], NEG) for k in range(nl // 4)]
        m = masked[0]
        for k in range(1, nl // 4):
            m = jnp.maximum(m, masked[k])
        m = jnp.max(m, axis=1, keepdims=True)
        weights = [jnp.where(x > 0.5 * NEG, jnp.exp2(x - m), 0.0) for x in masked]
        t = weights[0]
        for k in range(1, nl // 4):
            t = t + weights[k]
        t = jnp.sum(t, axis=1, keepdims=True)
        weights = jnp.concatenate(weights, axis=1).astype(BF16)
        data = er[:, i * slots:(i + 1) * slots, :].reshape(nl * slots, HD)
        o = jnp.dot(weights, data, preferred_element_type=F32) / jnp.maximum(t, 1e-30)
        ff[:, i * 8:(i + 1) * 8, :] = o.reshape(ng, 8, HD)
        lse = jnp.where(t > 0.0, m + jnp.log(jnp.maximum(t, 1e-30)) * LOG2E, NEG)
        lse_out = jnp.where(laneq == i, lse, lse_out)
    hi, mid, lo = pieces_of(lse_out)
    for k, piece in enumerate((hi, mid, lo, jnp.zeros_like(lo))):
        ff[:, 64 + 8 * k:72 + 8 * k, :] = piece.reshape(ng, 8, 128)
    fb[...] = ff[...].astype(BF16)
    fr[g] = fb[g]

    def send_f(k):
        gg = lax.rem(g + k, ng)
        copy(fb.at[gg], fr.at[g], S_F, gg, l).start()
    each(ng, send_f, far=True)

    wait_all(fr.at[pl.ds(0, ng - 1)], recv.at[S_F])
    data = [fr[gg].astype(F32) for gg in range(ng)]
    logs = [x[64:72] + x[72:80] + x[80:88] for x in data]
    for s in range(steps):
        pieces = []
        for j in range(4):
            i = s * 4 + j
            parts = [(logs[gg][:, i:i + 1], data[gg][i * 8:(i + 1) * 8]) for gg in range(ng)]
            parts += [(fresh_scores[i][t], fresh_v[t * 8:(t + 1) * 8]) for t in range(s + 1)]
            m = parts[0][0]
            for score, unused in parts[1:]:
                m = jnp.maximum(m, score)
            total = jnp.zeros((8, 1), F32)
            o = jnp.zeros((8, HD), F32)
            for score, value in parts:
                w = jnp.exp2(score - m)
                total = total + w
                o = o + w * value
            pieces.append(o / total)
        out[s] = jnp.concatenate(pieces, axis=1).astype(BF16)

    wait_all(wkv_v.at[pl.ds(0, (nl - 1) * kvrows)], send.at[S_KVW])
    wait_all(rs.at[pl.ds(0, nch - 1)], send.at[S_RS])
    wait_all(frs.at[pl.ds(0, ng - 1)], send.at[S_FRS])
    wait_all(er.at[pl.ds(0, nl - 1), pl.ds(0, 16 * SPLIT)], send.at[S_G1])
    wait_all(er.at[pl.ds(0, ny - 1), pl.ds(0, 16 * (4 - SPLIT))], send.at[S_G2])
    wait_all(q_all.at[:, pl.ds(0, ny - 1), 0, :, pl.ds(0, SPLIT)], send.at[S_H1])
    wait_all(er.at[pl.ds(0, nl - 1), pl.ds(0, 16 * ny * (4 - SPLIT))], send.at[S_H2])
    wait_all(q_all.at[:, :, 0], send.at[S_SIB])
    for kind in range(2):
        for pp in range(2):
            @pl.when((which == kind) & ((l % kvh) * 2 + pp != l))
            def _():
                wait_all(kvown, send.at[S_KEY + kind])
    wait_all(er.at[pl.ds(0, nl - 1)], send.at[S_E])
    wait_all(fr.at[pl.ds(0, ng - 1)], send.at[S_F])


def per_device(ng, nl, tokens, query_weight, kv_weight, pages, slot_request, slot_len):
    steps, req, width = tokens.shape
    rows = query_weight.shape[0]
    slots, unused, page, kvwidth = pages.shape
    kvh = kvwidth // HD
    ny = ng // CORES
    hbm = pl.BlockSpec(memory_space=pl.ANY)
    smem = pl.BlockSpec(memory_space=pltpu.SMEM)
    scratch = [
        pltpu.VMEM((steps, req, rows), BF16),
        pltpu.VMEM((rows, 4 * HD), BF16),
        pltpu.VMEM((rows, HD), BF16),
        pltpu.VMEM(pages.shape, BF16),
        pltpu.VMEM((2 * ng, 8, 4 * HD), F32),
        pltpu.VMEM((2 * ng, 8, 4 * HD), F32),
        pltpu.VMEM((steps, req, HD), F32),
        pltpu.VMEM((ng, steps, 8, HD), F32),
        pltpu.VMEM((steps * 8, HD), BF16),
        pltpu.VMEM((2, steps * 8, HD), BF16),
        pltpu.VMEM((kvh, ny, 2, 2, 4, 16, HD), BF16),
        pltpu.VMEM((16 * slots, HD), F32),
        pltpu.VMEM((nl, 8 * slots + 16, HD), BF16),
        pltpu.VMEM((nl, 8 * slots + 16, HD), BF16),
        pltpu.VMEM((ng, 96, HD), F32),
        pltpu.VMEM((ng, 96, HD), BF16),
        pltpu.VMEM((ng, 96, HD), BF16),
        pltpu.VMEM((128, HD), F32),
        pltpu.VMEM((ny, 2, 2, 4, 16, HD), BF16),
        pltpu.SemaphoreType.DMA((12,)),
        pltpu.SemaphoreType.DMA((12,)),
        pltpu.SemaphoreType.DMA((4, kvh)),
        pltpu.SemaphoreType.DMA((4,)),
    ]
    return pl.pallas_call(
        functools.partial(kernel, ng, nl),
        out_shape=jax.ShapeDtypeStruct((steps, req // ng, 4 * HD), BF16),
        in_specs=[hbm, hbm, hbm, hbm, smem, smem],
        out_specs=pl.BlockSpec(memory_space=pltpu.VMEM),
        scratch_shapes=scratch,
        compiler_params=pltpu.CompilerParams(
            collective_id=0, has_side_effects=True, vmem_limit_bytes=62 * 1024 * 1024),
    )(tokens, query_weight, kv_weight, pages, slot_request, slot_len)


def solution(mesh):
    ng, nl = mesh.shape["group"], mesh.shape["lend"]
    return jax.shard_map(
        functools.partial(per_device, ng, nl),
        mesh=mesh,
        in_specs=(
            P(),
            P("group", "lend"),
            P(("group", "lend"), None),
            P(("group", "lend"), None, None, None),
            P(("group", "lend")),
            P(("group", "lend")),
        ),
        out_specs=P(None, "group", "lend"),
        check_vma=False,
    )
```
